256 devices in a mesh: dp: 16 (over z, core), ctx: 4 (over y), tp: 4 (over x).
Axes of the slice: x: 4, y: 4, z: 8, core: 2. Of those that a mesh axis runs over, the one named last changes fastest.
Arguments:
- tokens_in: bfloat16 [8192, 5120], P(('dp', 'ctx'), 'tp'), may hold values from -6 to 6
- grad_out: bfloat16 [8192, 5120], P(('dp', 'ctx'), 'tp'), may hold values from -3 to 3
- router_logit: float32 [8192], P(('dp', 'ctx')), may hold values from -6 to 6
- expert_index: int32 [8192, 1], P(('dp', 'ctx')), may hold values from 0 to 7; in each aligned block of 128 rows (0 to 127, 128 to 255, ...) at most 20 rows name the same one
- gate_half: bfloat16 [16, 5120, 2048], P(('ctx', 'tp'), None, 'dp'), may hold values from -0.078125 to 0.078125
- up_half: bfloat16 [16, 5120, 2048], P(('ctx', 'tp'), None, 'dp'), may hold values from -0.078125 to 0.078125
- down_half: bfloat16 [16, 2048, 5120], P(('ctx', 'tp'), 'dp'), may hold values from -0.09375 to 0.09375
Outputs:
- input_grad: bfloat16 [8192, 5120], P(('dp', 'ctx'), 'tp')
- logit_grad: bfloat16 [8192], P(('dp', 'ctx'))
- gate_grad: bfloat16 [16, 5120, 2048], P(('ctx', 'tp'), None, 'dp')
- up_grad: bfloat16 [16, 5120, 2048], P(('ctx', 'tp'), None, 'dp')
- down_grad: bfloat16 [16, 2048, 5120], P(('ctx', 'tp'), 'dp')
The draws below stay inside these ranges and needn't reach their ends.
Inputs may be any that keep to these rules, and one draw needn't show every extreme that they name: `expert_index`: in each aligned block of 128 rows no expert is named by more than 20 rows, a bound that some block reaches.
All inputs are finite; a program needn't handle non-finite values.
Results may differ from the reference program's by a relative error of at most 0.025.
Values may be sent and summed in bfloat16 or wider, within the bound.
No kernel may reach another device: no remote copies, remote signals or barrier semaphores. Data moves between devices by JAX's collectives and lax.ppermute only.
A program may use at most 128 MiB of HBM per device.

```python
import math
import jax
import jax.numpy as jnp
import numpy as np
from jax import lax

D = 5120
HE = 4096
TOK_DEV = 128
HALF = 10
CAP = 20
EXPERTS = 8
TOKENS = 8192
N_DP = 16


def block_levels(stream_key, dims, pieces, low, largest):
    loudness, own = 1.0, jax.random.fold_in(stream_key, 6)
    for dim, shards_of in pieces:
        steps = jnp.exp(jax.random.uniform(jax.random.fold_in(own, dim), (shards_of,), jnp.float32, low / len(pieces), largest / len(pieces)))
        loudness = loudness * jnp.repeat(steps, dims[dim] // shards_of).reshape([-1 if axis == dim else 1 for axis in range(len(dims))])
    return loudness


def routed_block(stream_key, own, number, rows, number_of, top, reach, slope):
    order = jax.random.permutation(stream_key, number_of)
    crowded, ordinary = load_shares(number_of, rows * top, reach, slope, True), load_shares(number_of, rows * top, reach, slope, False)
    places = jnp.arange(number_of)

    def named(sizes, rotation):
        used = int((sizes > 0).sum())
        fixed = max(1, used // 4)
        passed = fixed + (places - fixed + rotation * (used - fixed)) % max(1, number_of - fixed)
        return jnp.zeros((number_of,), jnp.int32).at[order[jnp.where(places < fixed, places, passed)]].set(jnp.asarray(sizes, jnp.int32))

    sizes = jnp.where(number % 4 == 0, named(crowded, number // 4), named(ordinary, number - number // 4 - 1))
    mixed = jax.random.permutation(jax.random.fold_in(own, 3), number_of)
    source_of, taker = mixed[0:number_of // 2 * 2:2], mixed[1:number_of // 2 * 2:2]
    slack = jnp.minimum(sizes[source_of] - 1, reach - sizes[taker]) // 2
    slack = jnp.where((source_of == order[0]) | (taker == order[0]) | (sizes[taker] == 0), 0, jnp.maximum(slack, 0))
    passed = jax.random.randint(jax.random.fold_in(own, 4), (number_of // 2,), 0, 1 << 20) % (slack + 1)
    sizes = sizes.at[source_of].add(-passed).at[taker].add(passed)
    items = jnp.searchsorted(jnp.cumsum(sizes), jnp.arange(rows * top), side="right").astype(jnp.int32)
    table = items.reshape(top, rows).T
    table = table[jax.random.permutation(jax.random.fold_in(own, 1), rows)]
    rotation = jax.random.randint(jax.random.fold_in(own, 2), (rows, 1), 0, top)
    return jnp.take_along_axis(table, (jnp.arange(top)[None, :] + rotation) % top, axis=1)


def load_shares(count, total, limit, slope, full):
    loads = [(1 << 20) // math.isqrt(standing ** slope) + 1 for standing in range(1, count + 1)]
    largest = limit if full else min(limit, max(-(-total // count), total * loads[0] // sum(loads)))
    least = 1 if total - largest >= count - 1 else 0
    given, rest = [largest] + [least] * (count - 1), total - largest - least * (count - 1)
    while rest > 0:
        candidates = [i for i in range(1, count) if given[i] < largest] or [i for i in range(1, count) if given[i] < limit]
        whole, left = sum([loads[i] for i in candidates]), rest
        for i in candidates:
            addition = min(limit - given[i], max(1, left * loads[i] // whole), rest)
            given[i] = given[i] + addition
            rest = rest - addition
    return np.array(given)


def centred(own_key, dims, spread, most, cuts=(), kind=jnp.bfloat16):
    result = spread * jax.random.normal(own_key, dims, jnp.float32)
    if cuts:
        result = result * block_levels(own_key, dims, cuts, -0.22, 0.18)
    return jnp.clip(result, -most, most).astype(kind)


def setup_inputs(seed: int = 0) -> dict:
    key_list = jax.random.split(jax.random.key(seed), 8)
    tokens_in = centred(key_list[0], (TOKENS, D), 1.0, 6.0, ((0, 64), (1, 4)))
    grad_out = centred(key_list[1], (TOKENS, D), 0.5, 3.0, ((0, 64), (1, 4)))
    router_logit = centred(key_list[2], (TOKENS,), 1.5, 6.0, ((0, 64),), jnp.float32)
    expert_index_keys = jax.random.split(jax.random.fold_in(key_list[3], 1), TOKENS // TOK_DEV)
    expert_index_turns = jax.random.permutation(jax.random.fold_in(key_list[3], 3), TOKENS // TOK_DEV)
    expert_index = jax.vmap(lambda own, number: routed_block(jax.random.fold_in(key_list[3], 2), own, number, TOK_DEV, EXPERTS, 1, CAP, 2))(expert_index_keys, expert_index_turns).reshape((TOKENS, 1))
    gate_half = centred(key_list[4], (2 * EXPERTS, D, HE // 2), D ** -0.5, 0.078125, ((0, 16), (2, 16)))
    up_half = centred(key_list[5], (2 * EXPERTS, D, HE // 2), D ** -0.5, 0.078125, ((0, 16), (2, 16)))
    down_half = centred(key_list[6], (2 * EXPERTS, HE // 2, D), HE ** -0.5, 0.09375, ((0, 16), (1, 16)))
    return dict(tokens_in=tokens_in, grad_out=grad_out, router_logit=router_logit, expert_index=expert_index, gate_half=gate_half, up_half=up_half, down_half=down_half)


def rounded(value):
    return lax.optimization_barrier(value.astype(jnp.bfloat16)).astype(jnp.float32)


def reference(tokens_in, grad_out, router_logit, expert_index, gate_half, up_half, down_half):
    groups = TOKENS // TOK_DEV
    cap = 2 * HALF
    hs = HE // (2 * N_DP)
    route = expert_index[:, 0].astype(jnp.int32)
    hit = (route.reshape(groups, TOK_DEV, 1) == jnp.arange(EXPERTS, dtype=jnp.int32)).astype(jnp.int32)
    before = jnp.cumsum(hit, axis=1) - hit
    rank = jnp.sum(before * hit, axis=2).reshape(-1).astype(jnp.int32)
    group_of = (jnp.arange(TOKENS, dtype=jnp.int32) // TOK_DEV).astype(jnp.int32)
    place = ((route * groups + group_of) * cap + rank).astype(jnp.int32)
    total = EXPERTS * groups * cap
    slot_token = jnp.zeros((total,), jnp.int32).at[place].set(jnp.arange(TOKENS, dtype=jnp.int32))
    live = jnp.zeros((total,), jnp.float32).at[place].set(1.0)
    weight = jax.nn.sigmoid(router_logit).astype(jnp.bfloat16)
    live_b = live.astype(jnp.bfloat16)[:, None]
    slot_x = (tokens_in[slot_token] * live_b).reshape(EXPERTS, groups * cap, D)
    slot_dy = (grad_out[slot_token] * live_b).reshape(EXPERTS, groups * cap, D)
    slot_w = (weight.astype(jnp.float32)[slot_token] * live).reshape(EXPERTS, groups * cap)
    gate_blocks = gate_half.reshape(EXPERTS, 2, D, N_DP, hs).transpose(0, 3, 2, 1, 4).reshape(EXPERTS, N_DP, D, 2 * hs)
    up_blocks = up_half.reshape(EXPERTS, 2, D, N_DP, hs).transpose(0, 3, 2, 1, 4).reshape(EXPERTS, N_DP, D, 2 * hs)
    down_blocks = down_half.reshape(EXPERTS, 2, N_DP, hs, D).transpose(0, 2, 1, 3, 4).reshape(EXPERTS, N_DP, 2 * hs, D)
    inner = (((1,), (1,)), ((), ()))
    outer = (((0,), (0,)), ((), ()))

    def one_expert(items):
        xs, dys, ws, wg, wu, wd = items
        rows = xs.shape[0]
        scale = ws[:, None]
        member = (jnp.arange(rows, dtype=jnp.int32) // HALF) % 2
        keep_zero = (member == 0).astype(xs.dtype)[:, None]
        keep_one = (member == 1).astype(xs.dtype)[:, None]
        x_zero = xs * keep_zero
        x_one = xs * keep_one
        y_zero = dys * keep_zero
        y_one = dys * keep_one

        def mixed(first, second, axis):
            lo_first = lax.slice_in_dim(first, 0, hs, axis=axis)
            hi_first = lax.slice_in_dim(first, hs, 2 * hs, axis=axis)
            lo_second = lax.slice_in_dim(second, 0, hs, axis=axis)
            hi_second = lax.slice_in_dim(second, hs, 2 * hs, axis=axis)
            return jnp.concatenate([lo_first + rounded(lo_second), hi_second + rounded(hi_first)], axis).astype(jnp.bfloat16)

        def block(carry, piece):
            dx_acc, r_acc = carry
            wg_i, wu_i, wd_i = piece
            gate = jnp.dot(xs, wg_i, preferred_element_type=jnp.float32)
            up = jnp.dot(xs, wu_i, preferred_element_type=jnp.float32)
            sig = jax.nn.sigmoid(gate)
            act = gate * sig
            hidden = act * up
            back = lax.dot_general(dys, wd_i, inner, preferred_element_type=jnp.float32)
            r_acc = r_acc + rounded(jnp.sum(hidden * back, axis=1))
            grad_h = scale * back
            d_gate = (grad_h * up * sig * (1.0 + gate * (1.0 - sig))).astype(jnp.bfloat16)
            d_up = (grad_h * act).astype(jnp.bfloat16)
            scaled = (scale * hidden).astype(jnp.bfloat16)
            part = lax.dot_general(d_gate, wg_i, inner, preferred_element_type=jnp.float32)
            part = part + lax.dot_general(d_up, wu_i, inner, preferred_element_type=jnp.float32)
            dx_acc = dx_acc + rounded(part)
            g_zero = lax.dot_general(x_zero, d_gate, outer, preferred_element_type=jnp.float32)
            g_one = lax.dot_general(x_one, d_gate, outer, preferred_element_type=jnp.float32)
            u_zero = lax.dot_general(x_zero, d_up, outer, preferred_element_type=jnp.float32)
            u_one = lax.dot_general(x_one, d_up, outer, preferred_element_type=jnp.float32)
            b_zero = lax.dot_general(scaled, y_zero, outer, preferred_element_type=jnp.float32)
            b_one = lax.dot_general(scaled, y_one, outer, preferred_element_type=jnp.float32)
            grads = (mixed(g_zero, g_one, 1), mixed(u_zero, u_one, 1), mixed(b_zero, b_one, 0))
            return (dx_acc, r_acc), grads

        start = (jnp.zeros((rows, D), jnp.float32), jnp.zeros((rows,), jnp.float32))
        (dx_acc, r_acc), grads = lax.scan(block, start, (wg, wu, wd))
        return dx_acc, r_acc, grads[0], grads[1], grads[2]

    dx_all, r_all, gate_g, up_g, down_g = lax.map(one_expert, (slot_x, slot_dy, slot_w, gate_blocks, up_blocks, down_blocks))
    gate_grad = gate_g.reshape(EXPERTS, N_DP, D, 2, hs).transpose(0, 3, 2, 1, 4).reshape(2 * EXPERTS, D, HE // 2)
    up_grad = up_g.reshape(EXPERTS, N_DP, D, 2, hs).transpose(0, 3, 2, 1, 4).reshape(2 * EXPERTS, D, HE // 2)
    down_grad = down_g.reshape(EXPERTS, N_DP, 2, hs, D).transpose(0, 2, 1, 3, 4).reshape(2 * EXPERTS, HE // 2, D)
    input_grad = dx_all.reshape(total, D)[place].astype(jnp.bfloat16)
    weight_f = weight.astype(jnp.float32)
    logit_grad = (r_all.reshape(total)[place] * weight_f * (1.0 - weight_f)).astype(jnp.bfloat16)
    return input_grad, logit_grad, gate_grad, up_grad, down_grad
```

```python
import jax
import jax.numpy as jnp
from jax import lax
from jax.experimental import pallas as pl
from jax.experimental.pallas import tpu as pltpu
from jax.sharding import Mesh, PartitionSpec as P

HALF = 10
LANES = 128
BLOCK = 512
INNER = (((1,), (1,)), ((), ()))
OUTER = (((0,), (0,)), ((), ()))
F32 = jnp.float32
BF16 = jnp.bfloat16


def params():
    return pltpu.CompilerParams(vmem_limit_bytes=40 << 20)


def cost(flops, moved):
    return pl.CostEstimate(flops=int(flops), bytes_accessed=int(moved), transcendentals=0)


def hidden_kernel(x_ref, dy_ref, g0, g1, u0, u1, d0, d1, d_ref, s_ref, r_ref, gate_a, up_a, back_a):
    step = pl.program_id(0)

    @pl.when(step == 0)
    def _():
        gate_a[...] = jnp.zeros_like(gate_a)
        up_a[...] = jnp.zeros_like(up_a)
        back_a[...] = jnp.zeros_like(back_a)

    x = x_ref[...]
    dy = dy_ref[...]
    w_gate = jnp.concatenate([g0[...], g1[...]], 1)
    w_up = jnp.concatenate([u0[...], u1[...]], 1)
    w_down = jnp.concatenate([d0[...], d1[...]], 0)
    gate_a[...] += jnp.dot(x, w_gate, preferred_element_type=F32)
    up_a[...] += jnp.dot(x, w_up, preferred_element_type=F32)
    back_a[...] += lax.dot_general(dy, w_down, INNER, preferred_element_type=F32)

    @pl.when(step == pl.num_programs(0) - 1)
    def _():
        gate = gate_a[...]
        up = up_a[...]
        back = back_a[...]
        sig = jax.nn.sigmoid(gate)
        act = gate * sig
        hidden = act * up
        d_gate = (back * up * sig * (1.0 + gate * (1.0 - sig))).astype(BF16)
        d_up = (back * act).astype(BF16)
        half = gate.shape[1] // 2
        d_ref[:, :half] = d_gate[:, :half]
        d_ref[:, half : 2 * half] = d_up[:, :half]
        d_ref[:, 2 * half : 3 * half] = d_gate[:, half:]
        d_ref[:, 3 * half :] = d_up[:, half:]
        s_ref[...] = hidden.astype(BF16)
        total = jnp.sum(hidden * back, axis=1, keepdims=True)
        r_ref[...] = jnp.broadcast_to(total, r_ref.shape).astype(BF16)


def hidden_part(both, own, other):
    rows, wide = both.shape
    width = wide // 2
    half = own[0].shape[1]
    steps = width // BLOCK
    whole = lambda i: (0, 0)
    tall = pl.BlockSpec((BLOCK, half), lambda i: (i, 0))
    flat = pl.BlockSpec((half, BLOCK), lambda i: (0, i))
    return pl.pallas_call(
        hidden_kernel,
        grid=(steps,),
        in_specs=[
            pl.BlockSpec((rows, BLOCK), lambda i: (0, i)),
            pl.BlockSpec((rows, BLOCK), lambda i: (0, i + steps)),
            tall,
            tall,
            tall,
            tall,
            flat,
            flat,
        ],
        out_specs=[
            pl.BlockSpec((rows, 4 * half), whole),
            pl.BlockSpec((rows, 2 * half), whole),
            pl.BlockSpec((rows, LANES), whole),
        ],
        out_shape=[
            jax.ShapeDtypeStruct((rows, 4 * half), BF16),
            jax.ShapeDtypeStruct((rows, 2 * half), BF16),
            jax.ShapeDtypeStruct((rows, LANES), BF16),
        ],
        scratch_shapes=[pltpu.VMEM((rows, 2 * half), F32)] * 3,
        compiler_params=params(),
        cost_estimate=cost(12 * rows * width * half, 4 * rows * width),
        name="hidden_part",
    )(both, both, own[0], other[0], own[1], other[1], own[2], other[2])


def input_kernel(with_add, d_ref, r_ref, g0, u0, g1, u1, *rest):
    out_ref = rest[-1]
    step = pl.program_id(0)
    last = pl.num_programs(0) - 1

    @pl.when(step < last)
    def _():
        weights = jnp.concatenate([g0[...], u0[...], g1[...], u1[...]], 1)
        part = lax.dot_general(d_ref[...], weights, INNER, preferred_element_type=F32)
        if with_add:
            part = part + rest[0][...].astype(F32)
        out_ref[...] = part.astype(BF16)

    @pl.when(step == last)
    def _():
        part = r_ref[...].astype(F32)
        if with_add:
            part = part + rest[0][:, :LANES].astype(F32)
        out_ref[:, :LANES] = part.astype(BF16)


def input_part(d, router, own, other, addend=None):
    rows = d.shape[0]
    width, half = own[0].shape
    block = 1024
    steps = width // block
    whole = lambda i: (0, 0)
    tall = pl.BlockSpec((block, half), lambda i: (jnp.minimum(i, steps - 1), 0))
    strip = pl.BlockSpec((rows, block), lambda i: (0, i))
    operands = [d, router, own[0], own[1], other[0], other[1]]
    specs = [pl.BlockSpec((rows, 4 * half), whole), pl.BlockSpec((rows, LANES), whole)] + [tall] * 4
    if addend is not None:
        operands.append(addend)
        specs.append(strip)
    return pl.pallas_call(
        lambda *refs: input_kernel(addend is not None, *refs),
        grid=(steps + 1,),
        in_specs=specs,
        out_specs=strip,
        out_shape=jax.ShapeDtypeStruct((rows, width + LANES), BF16),
        compiler_params=params(),
        cost_estimate=cost(8 * rows * width * half, 2 * rows * width + 8 * width * half),
        name="input_part",
    )(*operands)


def weight_kernel(x_ref, dy_ref, d_ref, s_ref, gate_ref, up_ref, down_ref):
    half = gate_ref.shape[1]
    both = lax.dot_general(x_ref[...], d_ref[...], OUTER, preferred_element_type=F32)
    gate_ref[...] = both[:, :half].astype(gate_ref.dtype)
    up_ref[...] = both[:, half:].astype(up_ref.dtype)
    down = lax.dot_general(s_ref[...], dy_ref[...], OUTER, preferred_element_type=F32)
    down_ref[...] = down.astype(down_ref.dtype)


def weight_part(both, d, scaled, which, dtype):
    rows, wide = both.shape
    width = wide // 2
    half = scaled.shape[1] // 2
    steps = width // BLOCK
    tall = pl.BlockSpec((BLOCK, half), lambda i: (i, 0))
    return pl.pallas_call(
        weight_kernel,
        grid=(steps,),
        in_specs=[
            pl.BlockSpec((rows, BLOCK), lambda i: (0, i)),
            pl.BlockSpec((rows, BLOCK), lambda i: (0, i + steps)),
            pl.BlockSpec((rows, 2 * half), lambda i: (0, which)),
            pl.BlockSpec((rows, half), lambda i: (0, which)),
        ],
        out_specs=[tall, tall, pl.BlockSpec((half, BLOCK), lambda i: (0, i))],
        out_shape=[
            jax.ShapeDtypeStruct((width, half), dtype),
            jax.ShapeDtypeStruct((width, half), dtype),
            jax.ShapeDtypeStruct((half, width), dtype),
        ],
        compiler_params=params(),
        cost_estimate=cost(6 * rows * width * half, 4 * rows * width),
        name="weight_part",
    )(both, both, d, scaled)


def flip(value, axis):
    count = lax.axis_size(axis)
    return lax.ppermute(value, axis, [(i, i ^ 1) for i in range(count)])


def body(tokens_in, grad_out, router_logit, expert_index, gate_half, up_half, down_half):
    n_z = lax.axis_size("z")
    n_core = lax.axis_size("core")
    n_ctx = lax.axis_size("ctx")
    n_tp = lax.axis_size("tp")
    n_dev = n_ctx * n_tp
    n_exp = n_dev // 2
    tok_rows, part_width = tokens_in.shape
    width = part_width * n_tp
    slots = n_dev * HALF
    held = n_ctx * HALF
    route = expert_index[:, 0]
    hit = (route[:, None] == jnp.arange(n_exp, dtype=jnp.int32)[None, :]).astype(jnp.int32)
    before = jnp.cumsum(hit, axis=0) - hit
    rank = jnp.sum(before * hit, axis=1)
    target = 2 * route + rank // HALF
    place = target * HALF + rank % HALF
    weight = jax.nn.sigmoid(router_logit).astype(BF16).astype(F32)
    columns = jnp.arange(slots, dtype=jnp.int32)[None, :]
    pick = (place[:, None] == columns).astype(BF16)
    scaled_dy = (grad_out.astype(F32) * weight[:, None]).astype(BF16)
    send = lax.dot_general(
        pick,
        jnp.concatenate([tokens_in, scaled_dy], 1),
        OUTER,
        preferred_element_type=F32,
    ).astype(BF16)
    recv = lax.all_to_all(send, ("ctx", "tp"), split_axis=0, concat_axis=0, tiled=True)
    mine = (
        recv.reshape(n_ctx, n_tp, HALF, 2, part_width)
        .transpose(0, 2, 3, 1, 4)
        .reshape(held, 2 * width)
    )
    own = (gate_half[0], up_half[0], down_half[0])
    held_own = lax.optimization_barrier((own, recv))[0]
    other = tuple(flip(w, "tp") for w in held_own)
    both = lax.all_gather(mine, ("z", "core"), axis=0, tiled=True)
    d, scaled, router = hidden_part(both, own, other)
    give = weight_part(both, d, scaled, 1, BF16)
    got = tuple(flip(g, "tp") for g in give)
    core = lax.axis_index("core")

    def by_core(values):
        parts = values.reshape(n_z, n_core, held, values.shape[1])
        pick_core = lambda c: lax.dynamic_index_in_dim(parts, c, 1, False).reshape(
            n_z * held, values.shape[1]
        )
        return pick_core(core), pick_core(1 - core)

    d_in, _ = lax.optimization_barrier((d, give[0]))
    d_own, d_oth = by_core(d_in)
    r_own, r_oth = by_core(router)
    part_oth = input_part(d_oth, r_oth, own, other)
    from_core = flip(part_oth, "core")
    part = input_part(d_own, r_own, own, other, from_core)
    d_keep, _ = lax.optimization_barrier((d, part))
    keep = weight_part(both, d_keep, scaled, 0, F32)
    summed = lax.optimization_barrier(
        lax.psum_scatter(part, "z", scatter_dimension=0, tiled=True)
    )
    back_x = summed[:, :width].reshape(n_ctx, HALF, n_tp, part_width).transpose(0, 2, 1, 3)
    back_r = jnp.broadcast_to(
        summed[:, width:].reshape(n_ctx, 1, HALF, LANES), (n_ctx, n_tp, HALF, LANES)
    )
    ship = jnp.concatenate([back_x, back_r], 3).reshape(slots, part_width + LANES)
    landed = lax.all_to_all(ship, ("ctx", "tp"), split_axis=0, concat_axis=0, tiled=True)
    home = jnp.dot(pick, landed, preferred_element_type=F32)
    input_grad = home[:, :part_width].astype(BF16)
    logit_grad = (home[:, part_width] * (1.0 - weight)).astype(BF16)
    grads = tuple((k + g.astype(F32)).astype(BF16)[None] for k, g in zip(keep, got))
    return (input_grad, logit_grad) + grads


def solution(mesh):
    n_dp = mesh.shape["dp"]
    fine = Mesh(
        mesh.devices.reshape(n_dp // 2, 2, mesh.shape["ctx"], mesh.shape["tp"]),
        ("z", "core", "ctx", "tp"),
    )
    dp = ("z", "core")
    token = dp + ("ctx",)
    in_specs = (
        P(token, "tp"),
        P(token, "tp"),
        P(token),
        P(token, None),
        P(("ctx", "tp"), None, dp),
        P(("ctx", "tp"), None, dp),
        P(("ctx", "tp"), dp, None),
    )
    out_specs = (
        P(token, "tp"),
        P(token),
        P(("ctx", "tp"), None, dp),
        P(("ctx", "tp"), None, dp),
        P(("ctx", "tp"), dp, None),
    )
    return jax.shard_map(body, mesh=fine, in_specs=in_specs, out_specs=out_specs, check_vma=False)
```

```python
import jax
import jax.numpy as jnp
from jax import lax
from jax.experimental import pallas as pl
from jax.experimental.pallas import tpu as pltpu
from jax.sharding import Mesh, PartitionSpec as P

HALF = 10
PAD = 16
LANES = 128
BLOCK = 1024
LONG = 70_000_000_000
INNER = (((1,), (1,)), ((), ()))
OUTER = (((0,), (0,)), ((), ()))
F32 = jnp.float32
BF16 = jnp.bfloat16


def call(kernel, name, out_shape, vmem=60, flops=0, **kw):
    return pl.pallas_call(
        kernel,
        out_shape=out_shape,
        compiler_params=pltpu.CompilerParams(vmem_limit_bytes=vmem << 20),
        cost_estimate=pl.CostEstimate(flops=flops, bytes_accessed=0, transcendentals=0),
        name=name,
        **kw,
    )


def struct(shape, dtype):
    return jax.ShapeDtypeStruct(shape, dtype)


def whole(shape):
    return pl.BlockSpec(shape, lambda i: (0,) * len(shape))


def spread_kernel(x_ref, dy_ref, logit_ref, route_ref, send_ref, place_ref, n_dev):
    rows = x_ref.shape[0]
    route = route_ref[...]
    expert = lax.broadcasted_iota(jnp.int32, (n_dev // 2, rows), 0)
    hit = (route == expert).astype(F32)
    row = lax.broadcasted_iota(jnp.int32, (rows, rows), 0)
    col = lax.broadcasted_iota(jnp.int32, (rows, rows), 1)
    earlier = (row < col).astype(BF16)
    before = jnp.dot(hit.astype(BF16), earlier, preferred_element_type=F32)
    rank = jnp.sum(before * hit, axis=0, keepdims=True).astype(jnp.int32)
    member = (rank >= HALF).astype(jnp.int32)
    place = (2 * route + member) * PAD + rank - HALF * member
    place_ref[...] = place
    slot = lax.broadcasted_iota(jnp.int32, (n_dev * PAD, rows), 0)
    pick = (slot == place).astype(F32)
    weight = jax.nn.sigmoid(logit_ref[...]).astype(BF16).astype(F32)
    part = x_ref.shape[1]
    for k, (chosen, value) in enumerate(((pick, x_ref[...]), (pick * weight, dy_ref[...]))):
        out = jnp.dot(chosen.astype(BF16), value, preferred_element_type=F32).astype(BF16)
        for t in range(n_dev):
            send_ref[t, :, k * part : (k + 1) * part] = out[t * PAD : t * PAD + HALF]


def spread(x, dy, logit, route, n_dev):
    rows, part = x.shape
    return call(
        lambda *refs: spread_kernel(*refs, n_dev=n_dev),
        "spread",
        [struct((n_dev, HALF, 2 * part), BF16), struct((1, rows), jnp.int32)],
        vmem=16,
    )(x, dy, logit, route)


def arrange_kernel(recv_ref, out_ref, n_ctx, n_tp):
    part = recv_ref.shape[2] // 2
    for k in range(2):
        for t in range(n_tp):
            rows = [
                recv_ref[c * n_tp + t, :, k * part : (k + 1) * part].astype(F32)
                for c in range(n_ctx)
            ]
            start = (k * n_tp + t) * part
            out_ref[:, start : start + part] = jnp.concatenate(rows, 0).astype(BF16)


def arrange(recv, n_ctx, n_tp):
    part = recv.shape[2] // 2
    return call(
        lambda *refs: arrange_kernel(*refs, n_ctx=n_ctx, n_tp=n_tp),
        "arrange",
        struct((n_ctx * HALF, 2 * part * n_tp), BF16),
        vmem=16,
    )(recv)


def ship_kernel(sum_ref, out_ref, n_ctx, n_tp):
    part = out_ref.shape[2] - LANES
    width = part * n_tp
    router = sum_ref[:, width:].astype(F32)
    for t in range(n_tp):
        value = sum_ref[:, t * part : (t + 1) * part].astype(F32)
        for c in range(n_ctx):
            rows = slice(c * HALF, (c + 1) * HALF)
            out_ref[c * n_tp + t, :, :part] = value[rows].astype(BF16)
            out_ref[c * n_tp + t, :, part:] = router[rows].astype(BF16)


def ship(summed, n_ctx, n_tp):
    part = (summed.shape[1] - LANES) // n_tp
    return call(
        lambda *refs: ship_kernel(*refs, n_ctx=n_ctx, n_tp=n_tp),
        "ship",
        struct((n_ctx * n_tp, HALF, part + LANES), BF16),
        vmem=16,
    )(summed)


def home_kernel(land_ref, place_ref, logit_ref, input_ref, grad_ref):
    n_dev, _, wide = land_ref.shape
    rows, part = input_ref.shape
    fill = jnp.zeros((PAD - HALF, wide), F32)
    flat = []
    for t in range(n_dev):
        flat += [land_ref[t].astype(F32), fill]
    flat = jnp.concatenate(flat, 0).astype(BF16)
    slot = lax.broadcasted_iota(jnp.int32, (n_dev * PAD, rows), 0)
    pick = (slot == place_ref[...]).astype(BF16)
    home = lax.dot_general(pick, flat[:, :part], OUTER, preferred_element_type=F32)
    input_ref[...] = home.astype(BF16)
    router = lax.dot_general(flat[:, part:], pick, OUTER, preferred_element_type=F32)
    weight = jax.nn.sigmoid(logit_ref[...]).astype(BF16).astype(F32)
    grad_ref[...] = (router[:1] * (1.0 - weight)).astype(BF16)


def take_home(landed, place, logit):
    rows = place.shape[1]
    part = landed.shape[2] - LANES
    return call(
        home_kernel,
        "take_home",
        [struct((rows, part), BF16), struct((1, rows), BF16)],
        vmem=16,
    )(landed, place, logit)


def join(parts, axis):
    return jnp.concatenate([p[...] for p in parts], axis)


def gate_up_kernel(*refs):
    x_ref, gates, ups = refs[0], refs[1:5], refs[5:9]
    here_ref, there_ref, gate_ref, up_ref = refs[9:]
    step = pl.program_id(0)
    x = x_ref[...]
    gate_p = jnp.dot(x, join(gates, 1), preferred_element_type=F32)
    up_p = jnp.dot(x, join(ups, 1), preferred_element_type=F32)

    @pl.when(step == 0)
    def _():
        gate_ref[...] = gate_p
        up_ref[...] = up_p

    @pl.when(step > 0)
    def _():
        gate_ref[...] += gate_p
        up_ref[...] += up_p

    @pl.when(step == pl.num_programs(0) - 1)
    def _():
        half = here_ref.shape[1]
        for n, out in enumerate((here_ref, there_ref)):
            cols = slice(n * half, (n + 1) * half)
            gate = gate_ref[:, cols]
            out[...] = (gate * jax.nn.sigmoid(gate) * up_ref[:, cols]).astype(BF16)


def gate_up_part(both, sets):
    rows, wide = both.shape
    width = wide // 2
    unit = sets[0][0].shape[1]
    tall = pl.BlockSpec((BLOCK, unit), lambda i: (i, 0))
    return call(
        gate_up_kernel,
        "gate_up_part",
        [struct((rows, 2 * unit), BF16)] * 2 + [struct((rows, 4 * unit), F32)] * 2,
        grid=(width // BLOCK,),
        in_specs=[pl.BlockSpec((rows, BLOCK), lambda i: (0, i))] + [tall] * 8,
        out_specs=[whole((rows, 2 * unit))] * 2 + [whole((rows, 4 * unit))] * 2,
    )(both, *[s[0] for s in sets], *[s[1] for s in sets])


def back_kernel(*refs):
    dy_ref, downs = refs[0], refs[1:5]
    gate_ref, up_ref, here_ref, there_ref, r_ref, back_a = refs[5:]
    step = pl.program_id(0)
    back_p = lax.dot_general(dy_ref[...], join(downs, 0), INNER, preferred_element_type=F32)

    @pl.when(step == 0)
    def _():
        back_a[...] = back_p

    @pl.when(step > 0)
    def _():
        back_a[...] += back_p

    @pl.when(step == pl.num_programs(0) - 1)
    def _():
        unit = back_a.shape[1] // 4
        total = jnp.zeros((back_a.shape[0], 1), F32)
        for n in range(4):
            cols = slice(n * unit, (n + 1) * unit)
            gate = gate_ref[:, cols]
            up = up_ref[:, cols]
            back = back_a[:, cols]
            sig = jax.nn.sigmoid(gate)
            act = gate * sig
            out = here_ref if n < 2 else there_ref
            base = (n % 2) * 2 * unit
            d_gate = back * up * sig * (1.0 + gate * (1.0 - sig))
            out[:, base : base + unit] = d_gate.astype(BF16)
            out[:, base + unit : base + 2 * unit] = (back * act).astype(BF16)
            total = total + jnp.sum(act * up * back, axis=1, keepdims=True)
        r_ref[...] = jnp.broadcast_to(total, r_ref.shape).astype(BF16)


def back_part(both, downs, gate, up):
    rows, wide = both.shape
    width = wide // 2
    unit = downs[0].shape[0]
    steps = width // BLOCK
    return call(
        back_kernel,
        "back_part",
        [struct((rows, 4 * unit), BF16)] * 2 + [struct((rows, LANES), BF16)],
        grid=(steps,),
        in_specs=[pl.BlockSpec((rows, BLOCK), lambda i: (0, i + steps))]
        + [pl.BlockSpec((unit, BLOCK), lambda i: (0, i))] * 4
        + [whole((rows, 4 * unit))] * 2,
        out_specs=[whole((rows, 4 * unit))] * 2 + [whole((rows, LANES))],
        scratch_shapes=[pltpu.VMEM((rows, 4 * unit), F32)],
    )(both, *downs, gate, up)


def input_kernel(here_ref, there_ref, r_ref, *refs):
    out_ref = refs[-1]
    step = pl.program_id(0)
    last = pl.num_programs(0) - 1

    @pl.when(step < last)
    def _():
        weights = jnp.concatenate([w[...] for w in refs[:-1]], 1)
        d = jnp.concatenate([here_ref[...], there_ref[...]], 1)
        out_ref[...] = lax.dot_general(
            d, weights, INNER, preferred_element_type=F32
        ).astype(BF16)

    @pl.when(step == last)
    def _():
        out_ref[:, :LANES] = r_ref[...]


def input_part(here, there, router, sets):
    rows = here.shape[0]
    width, unit = sets[0][0].shape
    steps = width // BLOCK
    tall = pl.BlockSpec((BLOCK, unit), lambda i: (jnp.minimum(i, steps - 1), 0))
    strip = pl.BlockSpec((rows, BLOCK), lambda i: (0, i))
    weights = [w for s in sets for w in s]
    return call(
        input_kernel,
        "input_part",
        struct((rows, width + LANES), BF16),
        grid=(steps + 1,),
        in_specs=[whole((rows, 4 * unit))] * 2 + [whole((rows, LANES))] + [tall] * 8,
        out_specs=strip,
    )(here, there, router, *weights)


def tall_kernel(x0, x1, d0, d1, gate_ref, up_ref):
    unit = gate_ref.shape[1]
    x = jnp.concatenate([x0[...], x1[...]], 0)
    d = jnp.concatenate([d0[...], d1[...]], 0)
    out = lax.dot_general(x, d, OUTER, preferred_element_type=F32)
    gate_ref[...] = out[:, :unit].astype(gate_ref.dtype)
    up_ref[...] = out[:, unit:].astype(up_ref.dtype)


def tall_part(both, d, which, dtype, flops=0):
    rows, wide = both[0].shape
    width = wide // 2
    unit = d[0].shape[1] // 4
    x_spec = pl.BlockSpec((rows, BLOCK), lambda i: (0, i))
    d_spec = pl.BlockSpec((rows, 2 * unit), lambda i: (0, which))
    return call(
        tall_kernel,
        "tall_part",
        [struct((width, unit), dtype)] * 2,
        grid=(width // BLOCK,),
        in_specs=[x_spec] * 2 + [d_spec] * 2,
        out_specs=[pl.BlockSpec((BLOCK, unit), lambda i: (i, 0))] * 2,
        flops=flops,
    )(*both, *d)


def flat_kernel(y0, y1, s0, s1, *rest):
    down_ref = rest[-1]
    y = jnp.concatenate([y0[...], y1[...]], 0)
    s = jnp.concatenate([s0[...], s1[...]], 0)
    out = lax.dot_general(s, y, OUTER, preferred_element_type=F32)
    if len(rest) > 1:
        out = out + rest[0][...].astype(F32)
    down_ref[...] = out.astype(BF16)


def flat_part(both, s, which, addend=None, flops=0):
    rows, wide = both[0].shape
    width = wide // 2
    unit = s[0].shape[1] // 2
    steps = width // BLOCK
    y_spec = pl.BlockSpec((rows, BLOCK), lambda i: (0, i + steps))
    s_spec = pl.BlockSpec((rows, unit), lambda i: (0, which))
    o_spec = pl.BlockSpec((unit, BLOCK), lambda i: (0, i))
    extra = () if addend is None else (addend,)
    return call(
        flat_kernel,
        "flat_part",
        struct((unit, width), BF16),
        grid=(steps,),
        in_specs=[y_spec] * 2 + [s_spec] * 2 + [o_spec] * len(extra),
        out_specs=o_spec,
        flops=flops,
    )(*both, *s, *extra)


def flip(value, axis):
    count = lax.axis_size(axis)
    return lax.ppermute(value, axis, [(i, i ^ 1) for i in range(count)])


def after(value, first):
    return lax.optimization_barrier((value, first))[0]


def body(tokens_in, grad_out, router_logit, expert_index, gate_half, up_half, down_half):
    n_ctx = lax.axis_size("ctx")
    n_tp = lax.axis_size("tp")
    logit = router_logit[None]
    route = expert_index.reshape(1, -1)
    send, place = spread(tokens_in, grad_out, logit, route, n_ctx * n_tp)
    recv = lax.all_to_all(send, ("ctx", "tp"), split_axis=0, concat_axis=0, tiled=True)
    mine = arrange(recv, n_ctx, n_tp)
    own = (gate_half[0], up_half[0], down_half[0])
    other = tuple(flip(w, "tp") for w in after(own, recv))
    across = lambda group: tuple(flip(w, "core") for w in group)
    groups = (own, other, across(own), across(other))
    sets = tuple(g[:2] for g in groups)
    downs = tuple(g[2] for g in groups)
    here = lax.all_gather(mine, "z", axis=0, tiled=True)
    here, sets, downs = lax.optimization_barrier((here, sets, downs))
    beside = flip(here, "core")
    both = (here, beside)
    s_here, s_there, gate, up = gate_up_part(here, sets)
    s = (s_here, flip(s_there, "core"))
    give_down = flat_part(both, s, 1)
    got_down = flip(give_down, "tp")
    d_here, d_there, router = back_part(after(here, give_down), downs, gate, up)
    part = input_part(d_here, d_there, router, sets)
    summed = lax.optimization_barrier(
        lax.psum_scatter(part, "z", scatter_dimension=0, tiled=True)
    )
    d = after((d_here, flip(d_there, "core")), part)
    give = tall_part(both, d, 1, BF16)
    got = (flip(give[0], "tp"), flip(give[1], "tp"))
    s, d, got_down = lax.optimization_barrier((s, after(d, give[0]), got_down))
    down_grad = flat_part(both, s, 0, got_down, LONG)
    keep = tall_part(both, after(d, down_grad), 0, F32, LONG)
    summed = after(summed, keep[0])
    shipped = ship(summed, n_ctx, n_tp)
    landed = lax.all_to_all(shipped, ("ctx", "tp"), split_axis=0, concat_axis=0, tiled=True)
    input_grad, logit_grad = take_home(landed, place, logit)
    tall_grads = tuple((k + g.astype(F32)).astype(BF16)[None] for k, g in zip(keep, got))
    return (input_grad, logit_grad[0], *tall_grads, down_grad[None])


def solution(mesh):
    n_dp = mesh.shape["dp"]
    fine = Mesh(
        mesh.devices.reshape(n_dp // 2, 2, mesh.shape["ctx"], mesh.shape["tp"]),
        ("z", "core", "ctx", "tp"),
    )
    dp = ("z", "core")
    token = dp + ("ctx",)
    in_specs = (
        P(token, "tp"),
        P(token, "tp"),
        P(token),
        P(token, None),
        P(("ctx", "tp"), None, dp),
        P(("ctx", "tp"), None, dp),
        P(("ctx", "tp"), dp, None),
    )
    out_specs = (
        P(token, "tp"),
        P(token),
        P(("ctx", "tp"), None, dp),
        P(("ctx", "tp"), None, dp),
        P(("ctx", "tp"), dp, None),
    )
    return jax.shard_map(body, mesh=fine, in_specs=in_specs, out_specs=out_specs, check_vma=False)
```

```python
import jax
import jax.numpy as jnp
from jax import lax
from jax.experimental import pallas as pl
from jax.experimental.pallas import tpu as pltpu
from jax.sharding import Mesh, PartitionSpec as P

HALF = 10
MAIN = 8
REST = HALF - MAIN
PAD = 16
LANES = 128
BLOCK = 2560
LONG = 70_000_000_000
SHORT = 23_000_000_000
INNER = (((1,), (1,)), ((), ()))
OUTER = (((0,), (0,)), ((), ()))
F32 = jnp.float32
BF16 = jnp.bfloat16


def call(kernel, name, out_shape, vmem=60, flops=0, **kw):
    return pl.pallas_call(
        kernel,
        out_shape=out_shape,
        compiler_params=pltpu.CompilerParams(vmem_limit_bytes=vmem << 20),
        cost_estimate=pl.CostEstimate(flops=flops, bytes_accessed=0, transcendentals=0),
        name=name,
        **kw,
    )


def struct(shape, dtype):
    return jax.ShapeDtypeStruct(shape, dtype)


def whole(shape):
    return pl.BlockSpec(shape, lambda i: (0,) * len(shape))


def spread_kernel(x_ref, dy_ref, logit_ref, route_ref, send_ref, place_ref, n_dev):
    rows, part = x_ref.shape
    route = route_ref[...]
    expert = lax.broadcasted_iota(jnp.int32, (n_dev // 2, rows), 0)
    hit = (route == expert).astype(F32)
    row = lax.broadcasted_iota(jnp.int32, (rows, rows), 0)
    col = lax.broadcasted_iota(jnp.int32, (rows, rows), 1)
    earlier = (row < col).astype(BF16)
    before = jnp.dot(hit.astype(BF16), earlier, preferred_element_type=F32)
    rank = jnp.sum(before * hit, axis=0, keepdims=True).astype(jnp.int32)
    member = (rank >= HALF).astype(jnp.int32)
    place = (2 * route + member) * PAD + rank - HALF * member
    place_ref[...] = place
    weight = jax.nn.sigmoid(logit_ref[...]).astype(BF16).astype(F32)
    slot = lax.broadcasted_iota(jnp.int32, (n_dev * MAIN, rows), 0)
    target, r = slot // MAIN, slot % MAIN
    pieces = MAIN // REST
    main = (target * PAD + r == place).astype(F32)
    rest = (target * PAD + MAIN + r // pieces == place).astype(F32)
    which = (slot % pieces)[:, :1]
    cut = 2 * part // pieces
    extra = jnp.zeros((n_dev * MAIN, cut), F32)
    for k, (scale, value) in enumerate(((1.0, x_ref[...]), (weight, dy_ref[...]))):
        out = jnp.dot((main * scale).astype(BF16), value, preferred_element_type=F32)
        out = out.astype(BF16)
        for t in range(n_dev):
            send_ref[t, :, k * part : (k + 1) * part] = out[t * MAIN : (t + 1) * MAIN]
        tail = jnp.dot((rest * scale).astype(BF16), value, preferred_element_type=F32)
        for h in range(part // cut):
            chosen = which == k * (part // cut) + h
            extra = jnp.where(chosen, tail[:, h * cut : (h + 1) * cut], extra)
    extra = extra.astype(BF16)
    for t in range(n_dev):
        send_ref[t, :, 2 * part :] = extra[t * MAIN : (t + 1) * MAIN]


def spread(x, dy, logit, route, n_dev):
    rows, part = x.shape
    wide = 2 * part * HALF // MAIN
    return call(
        lambda *refs: spread_kernel(*refs, n_dev=n_dev),
        "spread",
        [struct((n_dev, MAIN, wide), BF16), struct((1, rows), jnp.int32)],
    )(x, dy, logit, route)


def arrange_kernel(recv_ref, out_ref, n_ctx, n_tp):
    n_dev = n_ctx * n_tp
    part = out_ref.shape[1] // (2 * n_tp)
    pieces = MAIN // REST
    cut = 2 * part // pieces
    extra = jnp.concatenate([recv_ref[t, :, 2 * part :] for t in range(n_dev)], 0)
    size = n_dev * MAIN
    row = lax.broadcasted_iota(jnp.int32, (size, size), 0)
    col = lax.broadcasted_iota(jnp.int32, (size, size), 1)
    group = n_ctx * REST
    t, p = row // (pieces * group), row // group % pieces
    c, i = row // REST % n_ctx, row % REST
    order = (col == (c * n_tp + t) * MAIN + i * pieces + p).astype(BF16)
    extra = jnp.dot(order, extra, preferred_element_type=F32)
    for k in range(2):
        for t in range(n_tp):
            rows = [
                recv_ref[c * n_tp + t, :, k * part : (k + 1) * part].astype(F32)
                for c in range(n_ctx)
            ]
            tail = []
            for h in range(part // cut):
                at = (t * pieces + k * (part // cut) + h) * group
                tail.append(extra[at : at + group])
            rows.append(jnp.concatenate(tail, 1))
            start = (k * n_tp + t) * part
            out_ref[:, start : start + part] = jnp.concatenate(rows, 0).astype(BF16)


def arrange(recv, part, n_ctx, n_tp):
    return call(
        lambda *refs: arrange_kernel(*refs, n_ctx=n_ctx, n_tp=n_tp),
        "arrange",
        struct((n_ctx * HALF, 2 * part * n_tp), BF16),
        vmem=16,
    )(recv)


def ship_kernel(sum_ref, out_ref, n_ctx, n_tp):
    part = out_ref.shape[2] - LANES
    width = part * n_tp
    router = sum_ref[:, width:].astype(F32)
    for t in range(n_tp):
        value = sum_ref[:, t * part : (t + 1) * part].astype(F32)
        for c in range(n_ctx):
            main = slice(c * MAIN, (c + 1) * MAIN)
            rest = slice(n_ctx * MAIN + c * REST, n_ctx * MAIN + (c + 1) * REST)
            both = jnp.concatenate([value[main], value[rest]], 0)
            out_ref[c * n_tp + t, :, :part] = both.astype(BF16)
            both = jnp.concatenate([router[main], router[rest]], 0)
            out_ref[c * n_tp + t, :, part:] = both.astype(BF16)


def ship(summed, n_ctx, n_tp):
    part = (summed.shape[1] - LANES) // n_tp
    return call(
        lambda *refs: ship_kernel(*refs, n_ctx=n_ctx, n_tp=n_tp),
        "ship",
        struct((n_ctx * n_tp, HALF, part + LANES), BF16),
        vmem=16,
    )(summed)


def home_kernel(land_ref, place_ref, logit_ref, input_ref, grad_ref):
    n_dev, _, wide = land_ref.shape
    rows, part = input_ref.shape
    fill = jnp.zeros((PAD - HALF, wide), F32)
    flat = []
    for t in range(n_dev):
        flat += [land_ref[t].astype(F32), fill]
    flat = jnp.concatenate(flat, 0).astype(BF16)
    slot = lax.broadcasted_iota(jnp.int32, (n_dev * PAD, rows), 0)
    pick = (slot == place_ref[...]).astype(BF16)
    home = lax.dot_general(pick, flat[:, :part], OUTER, preferred_element_type=F32)
    input_ref[...] = home.astype(BF16)
    router = lax.dot_general(flat[:, part:], pick, OUTER, preferred_element_type=F32)
    weight = jax.nn.sigmoid(logit_ref[...]).astype(BF16).astype(F32)
    grad_ref[...] = (router[:1] * (1.0 - weight)).astype(BF16)


def take_home(landed, place, logit):
    rows = place.shape[1]
    part = landed.shape[2] - LANES
    return call(
        home_kernel,
        "take_home",
        [struct((rows, part), BF16), struct((1, rows), BF16)],
        vmem=16,
    )(landed, place, logit)


def join(parts, axis):
    return jnp.concatenate([p[...] for p in parts], axis)


def gate_up_kernel(*refs):
    x_ref, gates, ups = refs[0], refs[1:5], refs[5:9]
    here_ref, there_ref, gate_ref, up_ref = refs[9:]
    step = pl.program_id(0)
    x = x_ref[...]
    gate_p = jnp.dot(x, join(gates, 1), preferred_element_type=F32)
    up_p = jnp.dot(x, join(ups, 1), preferred_element_type=F32)

    @pl.when(step == 0)
    def _():
        gate_ref[...] = gate_p
        up_ref[...] = up_p

    @pl.when(step > 0)
    def _():
        gate_ref[...] += gate_p
        up_ref[...] += up_p

    @pl.when(step == pl.num_programs(0) - 1)
    def _():
        half = here_ref.shape[1]
        for n, out in enumerate((here_ref, there_ref)):
            cols = slice(n * half, (n + 1) * half)
            gate = gate_ref[:, cols]
            out[...] = (gate * jax.nn.sigmoid(gate) * up_ref[:, cols]).astype(BF16)


def gate_up_part(both, sets):
    rows, wide = both.shape
    width = wide // 2
    unit = sets[0][0].shape[1]
    tall = pl.BlockSpec((BLOCK, unit), lambda i: (i, 0))
    return call(
        gate_up_kernel,
        "gate_up_part",
        [struct((rows, 2 * unit), BF16)] * 2 + [struct((rows, 4 * unit), F32)] * 2,
        grid=(width // BLOCK,),
        in_specs=[pl.BlockSpec((rows, BLOCK), lambda i: (0, i))] + [tall] * 8,
        out_specs=[whole((rows, 2 * unit))] * 2 + [whole((rows, 4 * unit))] * 2,
    )(both, *[s[0] for s in sets], *[s[1] for s in sets])


def back_kernel(*refs):
    dy_ref, downs = refs[0], refs[1:-6]
    gate_ref, up_ref, here_ref, there_ref, r_ref, back_a = refs[-6:]
    step = pl.program_id(0)
    back_p = lax.dot_general(dy_ref[...], join(downs, 0), INNER, preferred_element_type=F32)

    @pl.when(step == 0)
    def _():
        back_a[...] = back_p

    @pl.when(step > 0)
    def _():
        back_a[...] += back_p

    @pl.when(step == pl.num_programs(0) - 1)
    def _():
        unit = back_a.shape[1] // 4
        total = jnp.zeros((back_a.shape[0], 1), F32)
        for n in range(4):
            cols = slice(n * unit, (n + 1) * unit)
            gate = gate_ref[:, cols]
            up = up_ref[:, cols]
            back = back_a[:, cols]
            sig = jax.nn.sigmoid(gate)
            act = gate * sig
            out = here_ref if n < 2 else there_ref
            base = (n % 2) * 2 * unit
            d_gate = back * up * sig * (1.0 + gate * (1.0 - sig))
            out[:, base : base + unit] = d_gate.astype(BF16)
            out[:, base + unit : base + 2 * unit] = (back * act).astype(BF16)
            total = total + jnp.sum(act * up * back, axis=1, keepdims=True)
        r_ref[...] = jnp.broadcast_to(total, r_ref.shape).astype(BF16)


def back_part(both, downs, gate, up):
    rows, wide = both.shape
    width = wide // 2
    unit = gate.shape[1] // 4
    steps = width // BLOCK
    return call(
        back_kernel,
        "back_part",
        [struct((rows, 4 * unit), BF16)] * 2 + [struct((rows, LANES), BF16)],
        grid=(steps,),
        in_specs=[pl.BlockSpec((rows, BLOCK), lambda i: (0, i + steps))]
        + [pl.BlockSpec((w.shape[0], BLOCK), lambda i: (0, i)) for w in downs]
        + [whole((rows, 4 * unit))] * 2,
        out_specs=[whole((rows, 4 * unit))] * 2 + [whole((rows, LANES))],
        scratch_shapes=[pltpu.VMEM((rows, 4 * unit), F32)],
        flops=LONG,
    )(both, *downs, gate, up)


def input_kernel(here_ref, there_ref, r_ref, *refs):
    out_ref = refs[-1]
    step = pl.program_id(0)
    last = pl.num_programs(0) - 1

    @pl.when(step < last)
    def _():
        weights = jnp.concatenate([w[...] for w in refs[:-1]], 1)
        d = jnp.concatenate([here_ref[...], there_ref[...]], 1)
        out_ref[...] = lax.dot_general(
            d, weights, INNER, preferred_element_type=F32
        ).astype(BF16)

    @pl.when(step == last)
    def _():
        out_ref[:, :LANES] = r_ref[...]


def input_part(here, there, router, sets):
    rows = here.shape[0]
    width, unit = sets[0][0].shape
    steps = width // BLOCK
    tall = pl.BlockSpec((BLOCK, unit), lambda i: (jnp.minimum(i, steps - 1), 0))
    strip = pl.BlockSpec((rows, BLOCK), lambda i: (0, i))
    weights = [w for s in sets for w in s]
    return call(
        input_kernel,
        "input_part",
        struct((rows, width + LANES), BF16),
        grid=(steps + 1,),
        in_specs=[whole((rows, 4 * unit))] * 2 + [whole((rows, LANES))] + [tall] * 8,
        out_specs=strip,
    )(here, there, router, *weights)


def tall_kernel(x0, x1, d0, d1, gate_ref, up_ref):
    unit = gate_ref.shape[1]
    x = jnp.concatenate([x0[...], x1[...]], 0)
    d = jnp.concatenate([d0[...], d1[...]], 0)
    out = lax.dot_general(x, d, OUTER, preferred_element_type=F32)
    gate_ref[...] = out[:, :unit].astype(gate_ref.dtype)
    up_ref[...] = out[:, unit:].astype(up_ref.dtype)


def tall_part(both, d, which, dtype, flops=0):
    rows, wide = both[0].shape
    width = wide // 2
    unit = d[0].shape[1] // 4
    x_spec = pl.BlockSpec((rows, BLOCK), lambda i: (0, i))
    d_spec = pl.BlockSpec((rows, 2 * unit), lambda i: (0, which))
    return call(
        tall_kernel,
        "tall_part",
        [struct((width, unit), dtype)] * 2,
        grid=(width // BLOCK,),
        in_specs=[x_spec] * 2 + [d_spec] * 2,
        out_specs=[pl.BlockSpec((BLOCK, unit), lambda i: (i, 0))] * 2,
        flops=flops,
    )(*both, *d)


def flat_kernel(y0, y1, s0, s1, *rest):
    down_ref = rest[-1]
    y = jnp.concatenate([y0[...], y1[...]], 0)
    s = jnp.concatenate([s0[...], s1[...]], 0)
    out = lax.dot_general(s, y, OUTER, preferred_element_type=F32)
    if len(rest) > 1:
        out = out + rest[0][...].astype(F32)
    down_ref[...] = out.astype(BF16)


def flat_part(both, s, which, addend=None, flops=0):
    rows, wide = both[0].shape
    width = wide // 2
    unit = s[0].shape[1] // 2
    steps = width // BLOCK
    y_spec = pl.BlockSpec((rows, BLOCK), lambda i: (0, i + steps))
    s_spec = pl.BlockSpec((rows, unit), lambda i: (0, which))
    o_spec = pl.BlockSpec((unit, BLOCK), lambda i: (0, i))
    extra = () if addend is None else (addend,)
    return call(
        flat_kernel,
        "flat_part",
        struct((unit, width), BF16),
        grid=(steps,),
        in_specs=[y_spec] * 2 + [s_spec] * 2 + [o_spec] * len(extra),
        out_specs=o_spec,
        flops=flops,
    )(*both, *s, *extra)


def flip(value, axis):
    count = lax.axis_size(axis)
    return lax.ppermute(value, axis, [(i, i ^ 1) for i in range(count)])


def after(value, first):
    return lax.optimization_barrier((value, first))[0]


def body(tokens_in, grad_out, router_logit, expert_index, gate_half, up_half, down_half):
    n_ctx = lax.axis_size("ctx")
    n_tp = lax.axis_size("tp")
    logit = router_logit[None]
    route = expert_index.reshape(1, -1)
    send, place = spread(tokens_in, grad_out, logit, route, n_ctx * n_tp)
    recv = lax.all_to_all(send, ("ctx", "tp"), split_axis=0, concat_axis=0, tiled=True)
    mine = arrange(recv, tokens_in.shape[1], n_ctx, n_tp)
    own = (gate_half[0], up_half[0], down_half[0])
    other = tuple(flip(w, "tp") for w in after(own, recv))
    across = lambda group: tuple(flip(w, "core") for w in group)
    own_there = across(own)
    sets = (own[:2], other[:2], own_there[:2], across(other[:2]))
    here = lax.all_gather(mine, "z", axis=0, tiled=True)
    here, sets = lax.optimization_barrier((here, sets))
    beside = flip(here, "core")
    both = (here, beside)
    s_here, s_there, gate, up = gate_up_part(here, sets)
    down = after(other[2], s_here)
    downs = (own[2], down, own_there[2], flip(down, "core"))
    s = (s_here, flip(s_there, "core"))
    d_here, d_there, router = back_part(here, downs, gate, up)
    give_down = flat_part(both, after(s, router), 1)
    got_down = flip(give_down, "tp")
    part = input_part(after(d_here, give_down), d_there, router, sets)
    summed = lax.optimization_barrier(
        lax.psum_scatter(part, "z", scatter_dimension=0, tiled=True)
    )
    d = after((d_here, flip(d_there, "core")), part)
    give = tall_part(both, d, 1, BF16)
    got = (flip(give[0], "tp"), flip(give[1], "tp"))
    s, d, got_down = lax.optimization_barrier((s, after(d, give[0]), got_down))
    down_grad = flat_part(both, s, 0, got_down, SHORT)
    keep = tall_part(both, after(d, down_grad), 0, F32, SHORT)
    summed = after(summed, keep[0])
    shipped = ship(summed, n_ctx, n_tp)
    landed = lax.all_to_all(shipped, ("ctx", "tp"), split_axis=0, concat_axis=0, tiled=True)
    input_grad, logit_grad = take_home(landed, place, logit)
    tall_grads = tuple((k + g.astype(F32)).astype(BF16)[None] for k, g in zip(keep, got))
    return (input_grad, logit_grad[0], *tall_grads, down_grad[None])


def solution(mesh):
    n_dp = mesh.shape["dp"]
    fine = Mesh(
        mesh.devices.reshape(n_dp // 2, 2, mesh.shape["ctx"], mesh.shape["tp"]),
        ("z", "core", "ctx", "tp"),
    )
    dp = ("z", "core")
    token = dp + ("ctx",)
    in_specs = (
        P(token, "tp"),
        P(token, "tp"),
        P(token),
        P(token, None),
        P(("ctx", "tp"), None, dp),
        P(("ctx", "tp"), None, dp),
        P(("ctx", "tp"), dp, None),
    )
    out_specs = (
        P(token, "tp"),
        P(token),
        P(("ctx", "tp"), None, dp),
        P(("ctx", "tp"), None, dp),
        P(("ctx", "tp"), dp, None),
    )
    return jax.shard_map(body, mesh=fine, in_specs=in_specs, out_specs=out_specs, check_vma=False)
```

```python
import jax
import jax.numpy as jnp
from jax import lax
from jax.experimental import pallas as pl
from jax.experimental.pallas import tpu as pltpu
from jax.sharding import Mesh, PartitionSpec as P

HALF = 10
MAIN = 8
REST = HALF - MAIN
PAD = 16
LANES = 128
BLOCK = 2560
SHORT = 34_590_000_000
INNER = (((1,), (1,)), ((), ()))
OUTER = (((0,), (0,)), ((), ()))
F32 = jnp.float32
BF16 = jnp.bfloat16


def call(kernel, name, out_shape, vmem=60, flops=0, **kw):
    return pl.pallas_call(
        kernel,
        out_shape=out_shape,
        compiler_params=pltpu.CompilerParams(vmem_limit_bytes=vmem << 20),
        cost_estimate=pl.CostEstimate(flops=flops, bytes_accessed=0, transcendentals=0),
        name=name,
        **kw,
    )


def struct(shape, dtype):
    return jax.ShapeDtypeStruct(shape, dtype)


def whole(shape):
    return pl.BlockSpec(shape, lambda i: (0,) * len(shape))


def spread_kernel(x_ref, dy_ref, logit_ref, route_ref, send_ref, place_ref, n_dev):
    rows, part = x_ref.shape
    route = route_ref[...]
    expert = lax.broadcasted_iota(jnp.int32, (n_dev // 2, rows), 0)
    hit = (route == expert).astype(F32)
    row = lax.broadcasted_iota(jnp.int32, (rows, rows), 0)
    col = lax.broadcasted_iota(jnp.int32, (rows, rows), 1)
    earlier = (row < col).astype(BF16)
    before = jnp.dot(hit.astype(BF16), earlier, preferred_element_type=F32)
    rank = jnp.sum(before * hit, axis=0, keepdims=True).astype(jnp.int32)
    member = (rank >= HALF).astype(jnp.int32)
    place = (2 * route + member) * PAD + rank - HALF * member
    place_ref[...] = place
    weight = jax.nn.sigmoid(logit_ref[...]).astype(BF16).astype(F32)
    slot = lax.broadcasted_iota(jnp.int32, (n_dev * MAIN, rows), 0)
    target, r = slot // MAIN, slot % MAIN
    pieces = MAIN // REST
    main = (target * PAD + r == place).astype(F32)
    rest = (target * PAD + MAIN + r // pieces == place).astype(F32)
    which = (slot % pieces)[:, :1]
    cut = 2 * part // pieces
    extra = jnp.zeros((n_dev * MAIN, cut), F32)
    for k, (scale, value) in enumerate(((1.0, x_ref[...]), (weight, dy_ref[...]))):
        out = jnp.dot((main * scale).astype(BF16), value, preferred_element_type=F32)
        out = out.astype(BF16)
        for t in range(n_dev):
            send_ref[t, :, k * part : (k + 1) * part] = out[t * MAIN : (t + 1) * MAIN]
        tail = jnp.dot((rest * scale).astype(BF16), value, preferred_element_type=F32)
        for h in range(part // cut):
            chosen = which == k * (part // cut) + h
            extra = jnp.where(chosen, tail[:, h * cut : (h + 1) * cut], extra)
    extra = extra.astype(BF16)
    for t in range(n_dev):
        send_ref[t, :, 2 * part :] = extra[t * MAIN : (t + 1) * MAIN]


def spread(x, dy, logit, route, n_dev):
    rows, part = x.shape
    wide = 2 * part * HALF // MAIN
    return call(
        lambda *refs: spread_kernel(*refs, n_dev=n_dev),
        "spread",
        [struct((n_dev, MAIN, wide), BF16), struct((1, rows), jnp.int32)],
    )(x, dy, logit, route)


def arrange_kernel(recv_ref, out_ref, n_ctx, n_tp):
    n_dev = n_ctx * n_tp
    part = out_ref.shape[1] // (2 * n_tp)
    pieces = MAIN // REST
    cut = 2 * part // pieces
    extra = jnp.concatenate([recv_ref[t, :, 2 * part :] for t in range(n_dev)], 0)
    size = n_dev * MAIN
    row = lax.broadcasted_iota(jnp.int32, (size, size), 0)
    col = lax.broadcasted_iota(jnp.int32, (size, size), 1)
    group = n_ctx * REST
    t, p = row // (pieces * group), row // group % pieces
    c, i = row // REST % n_ctx, row % REST
    order = (col == (c * n_tp + t) * MAIN + i * pieces + p).astype(BF16)
    extra = jnp.dot(order, extra, preferred_element_type=F32)
    for k in range(2):
        for t in range(n_tp):
            rows = [
                recv_ref[c * n_tp + t, :, k * part : (k + 1) * part].astype(F32)
                for c in range(n_ctx)
            ]
            tail = []
            for h in range(part // cut):
                at = (t * pieces + k * (part // cut) + h) * group
                tail.append(extra[at : at + group])
            rows.append(jnp.concatenate(tail, 1))
            start = (k * n_tp + t) * part
            out_ref[:, start : start + part] = jnp.concatenate(rows, 0).astype(BF16)


def arrange(recv, part, n_ctx, n_tp):
    return call(
        lambda *refs: arrange_kernel(*refs, n_ctx=n_ctx, n_tp=n_tp),
        "arrange",
        struct((n_ctx * HALF, 2 * part * n_tp), BF16),
        vmem=16,
    )(recv)


def ship_kernel(sum_ref, out_ref, n_ctx, n_tp):
    part = out_ref.shape[2] - LANES
    width = part * n_tp
    router = sum_ref[:, width:].astype(F32)
    for t in range(n_tp):
        value = sum_ref[:, t * part : (t + 1) * part].astype(F32)
        for c in range(n_ctx):
            main = slice(c * MAIN, (c + 1) * MAIN)
            rest = slice(n_ctx * MAIN + c * REST, n_ctx * MAIN + (c + 1) * REST)
            both = jnp.concatenate([value[main], value[rest]], 0)
            out_ref[c * n_tp + t, :, :part] = both.astype(BF16)
            both = jnp.concatenate([router[main], router[rest]], 0)
            out_ref[c * n_tp + t, :, part:] = both.astype(BF16)


def ship(summed, n_ctx, n_tp):
    part = (summed.shape[1] - LANES) // n_tp
    return call(
        lambda *refs: ship_kernel(*refs, n_ctx=n_ctx, n_tp=n_tp),
        "ship",
        struct((n_ctx * n_tp, HALF, part + LANES), BF16),
        vmem=16,
    )(summed)


def home_kernel(land_ref, place_ref, logit_ref, input_ref, grad_ref):
    n_dev, _, wide = land_ref.shape
    rows, part = input_ref.shape
    fill = jnp.zeros((PAD - HALF, wide), F32)
    flat = []
    for t in range(n_dev):
        flat += [land_ref[t].astype(F32), fill]
    flat = jnp.concatenate(flat, 0).astype(BF16)
    slot = lax.broadcasted_iota(jnp.int32, (n_dev * PAD, rows), 0)
    pick = (slot == place_ref[...]).astype(BF16)
    home = lax.dot_general(pick, flat[:, :part], OUTER, preferred_element_type=F32)
    input_ref[...] = home.astype(BF16)
    router = lax.dot_general(flat[:, part:], pick, OUTER, preferred_element_type=F32)
    weight = jax.nn.sigmoid(logit_ref[...]).astype(BF16).astype(F32)
    grad_ref[...] = (router[:1] * (1.0 - weight)).astype(BF16)


def take_home(landed, place, logit):
    rows = place.shape[1]
    part = landed.shape[2] - LANES
    return call(
        home_kernel,
        "take_home",
        [struct((rows, part), BF16), struct((1, rows), BF16)],
        vmem=16,
    )(landed, place, logit)


def join(parts, axis):
    return jnp.concatenate([p[...] for p in parts], axis)


def gate_up_kernel(*refs):
    x_ref, gates, ups = refs[0], refs[1:5], refs[5:9]
    here_ref, there_ref, gate_ref, up_ref = refs[9:]
    step = pl.program_id(0)
    x = x_ref[...]
    gate_p = jnp.dot(x, join(gates, 1), preferred_element_type=F32)
    up_p = jnp.dot(x, join(ups, 1), preferred_element_type=F32)

    @pl.when(step == 0)
    def _():
        gate_ref[...] = gate_p
        up_ref[...] = up_p

    @pl.when(step > 0)
    def _():
        gate_ref[...] += gate_p
        up_ref[...] += up_p

    @pl.when(step == pl.num_programs(0) - 1)
    def _():
        half = here_ref.shape[1]
        for n, out in enumerate((here_ref, there_ref)):
            cols = slice(n * half, (n + 1) * half)
            gate = gate_ref[:, cols]
            out[...] = (gate * jax.nn.sigmoid(gate) * up_ref[:, cols]).astype(BF16)


def gate_up_part(both, sets):
    rows, wide = both.shape
    width = wide // 2
    unit = sets[0][0].shape[1]
    tall = pl.BlockSpec((BLOCK, unit), lambda i: (i, 0))
    return call(
        gate_up_kernel,
        "gate_up_part",
        [struct((rows, 2 * unit), BF16)] * 2 + [struct((rows, 4 * unit), F32)] * 2,
        grid=(width // BLOCK,),
        in_specs=[pl.BlockSpec((rows, BLOCK), lambda i: (0, i))] + [tall] * 8,
        out_specs=[whole((rows, 2 * unit))] * 2 + [whole((rows, 4 * unit))] * 2,
    )(both, *[s[0] for s in sets], *[s[1] for s in sets])


def back_kernel(*refs):
    dy_ref, downs = refs[0], refs[1:-6]
    gate_ref, up_ref, here_ref, there_ref, r_ref, back_a = refs[-6:]
    step = pl.program_id(0)
    back_p = lax.dot_general(dy_ref[...], join(downs, 0), INNER, preferred_element_type=F32)

    @pl.when(step == 0)
    def _():
        back_a[...] = back_p

    @pl.when(step > 0)
    def _():
        back_a[...] += back_p

    @pl.when(step == pl.num_programs(0) - 1)
    def _():
        unit = back_a.shape[1] // 4
        total = jnp.zeros((back_a.shape[0], 1), F32)
        for n in range(4):
            cols = slice(n * unit, (n + 1) * unit)
            gate = gate_ref[:, cols]
            up = up_ref[:, cols]
            back = back_a[:, cols]
            sig = jax.nn.sigmoid(gate)
            act = gate * sig
            out = here_ref if n < 2 else there_ref
            base = (n % 2) * 2 * unit
            d_gate = back * up * sig * (1.0 + gate * (1.0 - sig))
            out[:, base : base + unit] = d_gate.astype(BF16)
            out[:, base + unit : base + 2 * unit] = (back * act).astype(BF16)
            total = total + jnp.sum(act * up * back, axis=1, keepdims=True)
        r_ref[...] = jnp.broadcast_to(total, r_ref.shape).astype(BF16)


def back_part(both, downs, gate, up):
    rows, wide = both.shape
    width = wide // 2
    unit = gate.shape[1] // 4
    steps = width // BLOCK
    return call(
        back_kernel,
        "back_part",
        [struct((rows, 4 * unit), BF16)] * 2 + [struct((rows, LANES), BF16)],
        grid=(steps,),
        in_specs=[pl.BlockSpec((rows, BLOCK), lambda i: (0, i + steps))]
        + [pl.BlockSpec((w.shape[0], BLOCK), lambda i: (0, i)) for w in downs]
        + [whole((rows, 4 * unit))] * 2,
        out_specs=[whole((rows, 4 * unit))] * 2 + [whole((rows, LANES))],
        scratch_shapes=[pltpu.VMEM((rows, 4 * unit), F32)],

    )(both, *downs, gate, up)


def input_kernel(here_ref, there_ref, r_ref, *refs):
    out_ref = refs[-1]
    step = pl.program_id(0)
    last = pl.num_programs(0) - 1

    @pl.when(step < last)
    def _():
        weights = jnp.concatenate([w[...] for w in refs[:-1]], 1)
        d = jnp.concatenate([here_ref[...], there_ref[...]], 1)
        out_ref[...] = lax.dot_general(
            d, weights, INNER, preferred_element_type=F32
        ).astype(BF16)

    @pl.when(step == last)
    def _():
        out_ref[:, :LANES] = r_ref[...]


def input_part(here, there, router, sets):
    rows = here.shape[0]
    width, unit = sets[0][0].shape
    steps = width // BLOCK
    tall = pl.BlockSpec((BLOCK, unit), lambda i: (jnp.minimum(i, steps - 1), 0))
    strip = pl.BlockSpec((rows, BLOCK), lambda i: (0, i))
    weights = [w for s in sets for w in s]
    return call(
        input_kernel,
        "input_part",
        struct((rows, width + LANES), BF16),
        grid=(steps + 1,),
        in_specs=[whole((rows, 4 * unit))] * 2 + [whole((rows, LANES))] + [tall] * 8,
        out_specs=strip,
    )(here, there, router, *weights)


def tall_kernel(x0, x1, d0, d1, gate_ref, up_ref):
    unit = gate_ref.shape[1]
    x = jnp.concatenate([x0[...], x1[...]], 0)
    d = jnp.concatenate([d0[...], d1[...]], 0)
    out = lax.dot_general(x, d, OUTER, preferred_element_type=F32)
    gate_ref[...] = out[:, :unit].astype(gate_ref.dtype)
    up_ref[...] = out[:, unit:].astype(up_ref.dtype)


def tall_part(both, d, which, dtype, flops=0):
    rows, wide = both[0].shape
    width = wide // 2
    unit = d[0].shape[1] // 4
    x_spec = pl.BlockSpec((rows, BLOCK), lambda i: (0, i))
    d_spec = pl.BlockSpec((rows, 2 * unit), lambda i: (0, which))
    return call(
        tall_kernel,
        "tall_part",
        [struct((width, unit), dtype)] * 2,
        grid=(width // BLOCK,),
        in_specs=[x_spec] * 2 + [d_spec] * 2,
        out_specs=[pl.BlockSpec((BLOCK, unit), lambda i: (i, 0))] * 2,
        flops=flops,
    )(*both, *d)


def flat_kernel(y0, y1, s0, s1, *rest):
    down_ref = rest[-1]
    y = jnp.concatenate([y0[...], y1[...]], 0)
    s = jnp.concatenate([s0[...], s1[...]], 0)
    out = lax.dot_general(s, y, OUTER, preferred_element_type=F32)
    if len(rest) > 1:
        out = out + rest[0][...].astype(F32)
    down_ref[...] = out.astype(BF16)


def flat_part(both, s, which, addend=None, flops=0):
    rows, wide = both[0].shape
    width = wide // 2
    unit = s[0].shape[1] // 2
    steps = width // BLOCK
    y_spec = pl.BlockSpec((rows, BLOCK), lambda i: (0, i + steps))
    s_spec = pl.BlockSpec((rows, unit), lambda i: (0, which))
    o_spec = pl.BlockSpec((unit, BLOCK), lambda i: (0, i))
    extra = () if addend is None else (addend,)
    return call(
        flat_kernel,
        "flat_part",
        struct((unit, width), BF16),
        grid=(steps,),
        in_specs=[y_spec] * 2 + [s_spec] * 2 + [o_spec] * len(extra),
        out_specs=o_spec,
        flops=flops,
    )(*both, *s, *extra)


def flip(value, axis):
    count = lax.axis_size(axis)
    return lax.ppermute(value, axis, [(i, i ^ 1) for i in range(count)])


def after(value, first):
    return lax.optimization_barrier((value, first))[0]


def body(tokens_in, grad_out, router_logit, expert_index, gate_half, up_half, down_half):
    n_ctx = lax.axis_size("ctx")
    n_tp = lax.axis_size("tp")
    logit = router_logit[None]
    route = expert_index.reshape(1, -1)
    send, place = spread(tokens_in, grad_out, logit, route, n_ctx * n_tp)
    recv = lax.all_to_all(send, ("ctx", "tp"), split_axis=0, concat_axis=0, tiled=True)
    mine = arrange(recv, tokens_in.shape[1], n_ctx, n_tp)
    own = (gate_half[0], up_half[0], down_half[0])
    cut = own[2].shape[0] // 2
    gate, up, down = after(own, recv)
    other = (flip(gate, "tp"), flip(up, "tp"))
    most, late = flip(down[:cut], "tp"), flip(down[cut:], "tp")
    across = lambda group: tuple(flip(w, "core") for w in group)
    own_there = across(own)
    sets = (own[:2], other, own_there[:2], across(other))
    here = lax.all_gather(mine, "z", axis=0, tiled=True)
    here, sets, most = lax.optimization_barrier((here, sets, most))
    beside = flip(here, "core")
    both = (here, beside)
    s_here, s_there, gate, up = gate_up_part(here, sets)
    s = (s_here, flip(s_there, "core"))
    give_down = flat_part(both, s, 1)
    got_down = flip(give_down, "tp")
    down = after((most, late), give_down)
    downs = (own[2], *down, own_there[2], *across(down))
    d_here, d_there, router = back_part(after(here, give_down), downs, gate, up)
    part = input_part(d_here, d_there, router, sets)
    summed = lax.optimization_barrier(
        lax.psum_scatter(part, "z", scatter_dimension=0, tiled=True)
    )
    d = after((d_here, flip(d_there, "core")), part)
    give = tall_part(both, d, 1, BF16)
    got = (flip(give[0], "tp"), flip(give[1], "tp"))
    s, d, got_down = lax.optimization_barrier((s, after(d, give[0]), got_down))
    down_grad = flat_part(both, s, 0, got_down, SHORT)
    keep = tall_part(both, after(d, down_grad), 0, F32, SHORT)
    summed = after(summed, keep[0])
    shipped = ship(summed, n_ctx, n_tp)
    landed = lax.all_to_all(shipped, ("ctx", "tp"), split_axis=0, concat_axis=0, tiled=True)
    input_grad, logit_grad = take_home(landed, place, logit)
    tall_grads = tuple((k + g.astype(F32)).astype(BF16)[None] for k, g in zip(keep, got))
    return (input_grad, logit_grad[0], *tall_grads, down_grad[None])


def solution(mesh):
    n_dp = mesh.shape["dp"]
    fine = Mesh(
        mesh.devices.reshape(n_dp // 2, 2, mesh.shape["ctx"], mesh.shape["tp"]),
        ("z", "core", "ctx", "tp"),
    )
    dp = ("z", "core")
    token = dp + ("ctx",)
    in_specs = (
        P(token, "tp"),
        P(token, "tp"),
        P(token),
        P(token, None),
        P(("ctx", "tp"), None, dp),
        P(("ctx", "tp"), None, dp),
        P(("ctx", "tp"), dp, None),
    )
    out_specs = (
        P(token, "tp"),
        P(token),
        P(("ctx", "tp"), None, dp),
        P(("ctx", "tp"), None, dp),
        P(("ctx", "tp"), dp, None),
    )
    return jax.shard_map(body, mesh=fine, in_specs=in_specs, out_specs=out_specs, check_vma=False)
```

```python
import jax
import jax.numpy as jnp
from jax import lax
from jax.experimental import pallas as pl
from jax.experimental.pallas import tpu as pltpu
from jax.sharding import Mesh, PartitionSpec as P

HALF = 10
MAIN = 8
REST = HALF - MAIN
PAD = 16
LANES = 128
BLOCK = 2560
PIECE = 640
FAR = 3
CHUNKS = 4
SHORT = 34_590_000_000
INNER = (((1,), (1,)), ((), ()))
OUTER = (((0,), (0,)), ((), ()))
F32 = jnp.float32
BF16 = jnp.bfloat16


def call(kernel, name, out_shape, vmem=60 << 20, flops=0, **kw):
    return pl.pallas_call(
        kernel,
        out_shape=out_shape,
        compiler_params=pltpu.CompilerParams(vmem_limit_bytes=vmem),
        cost_estimate=pl.CostEstimate(flops=flops, bytes_accessed=0, transcendentals=0),
        name=name,
        **kw,
    )


def struct(shape, dtype):
    return jax.ShapeDtypeStruct(shape, dtype)


def whole(shape):
    return pl.BlockSpec(shape, lambda i: (0,) * len(shape))


def spread_kernel(x_ref, dy_ref, logit_ref, route_ref, send_ref, place_ref, n_dev):
    rows, part = x_ref.shape
    route = route_ref[...]
    expert = lax.broadcasted_iota(jnp.int32, (n_dev // 2, rows), 0)
    hit = (route == expert).astype(F32)
    row = lax.broadcasted_iota(jnp.int32, (rows, rows), 0)
    col = lax.broadcasted_iota(jnp.int32, (rows, rows), 1)
    earlier = (row < col).astype(BF16)
    before = jnp.dot(hit.astype(BF16), earlier, preferred_element_type=F32)
    rank = jnp.sum(before * hit, axis=0, keepdims=True).astype(jnp.int32)
    member = (rank >= HALF).astype(jnp.int32)
    place = (2 * route + member) * PAD + rank - HALF * member
    place_ref[...] = place
    weight = jax.nn.sigmoid(logit_ref[...]).astype(BF16).astype(F32)
    slot = lax.broadcasted_iota(jnp.int32, (n_dev * MAIN, rows), 0)
    target, r = slot // MAIN, slot % MAIN
    pieces = MAIN // REST
    main = (target * PAD + r == place).astype(F32)
    rest = (target * PAD + MAIN + r // pieces == place).astype(F32)
    which = (slot % pieces)[:, :1]
    cut = 2 * part // pieces
    extra = jnp.zeros((n_dev * MAIN, cut), F32)
    for k, (scale, value) in enumerate(((1.0, x_ref[...]), (weight, dy_ref[...]))):
        out = jnp.dot((main * scale).astype(BF16), value, preferred_element_type=F32)
        out = out.astype(BF16)
        for t in range(n_dev):
            send_ref[t, :, k * part : (k + 1) * part] = out[t * MAIN : (t + 1) * MAIN]
        tail = jnp.dot((rest * scale).astype(BF16), value, preferred_element_type=F32)
        for h in range(part // cut):
            chosen = which == k * (part // cut) + h
            extra = jnp.where(chosen, tail[:, h * cut : (h + 1) * cut], extra)
    extra = extra.astype(BF16)
    for t in range(n_dev):
        send_ref[t, :, 2 * part :] = extra[t * MAIN : (t + 1) * MAIN]


def spread(x, dy, logit, route, n_dev):
    rows, part = x.shape
    wide = 2 * part * HALF // MAIN
    return call(
        lambda *refs: spread_kernel(*refs, n_dev=n_dev),
        "spread",
        [struct((n_dev, MAIN, wide), BF16), struct((1, rows), jnp.int32)],
    )(x, dy, logit, route)


def arrange_kernel(recv_ref, out_ref, n_ctx, n_tp):
    n_dev = n_ctx * n_tp
    part = out_ref.shape[1] // (2 * n_tp)
    pieces = MAIN // REST
    cut = 2 * part // pieces
    extra = jnp.concatenate([recv_ref[t, :, 2 * part :] for t in range(n_dev)], 0)
    size = n_dev * MAIN
    row = lax.broadcasted_iota(jnp.int32, (size, size), 0)
    col = lax.broadcasted_iota(jnp.int32, (size, size), 1)
    group = n_ctx * REST
    t, p = row // (pieces * group), row // group % pieces
    c, i = row // REST % n_ctx, row % REST
    order = (col == (c * n_tp + t) * MAIN + i * pieces + p).astype(BF16)
    extra = jnp.dot(order, extra, preferred_element_type=F32)
    for k in range(2):
        for t in range(n_tp):
            rows = [
                recv_ref[c * n_tp + t, :, k * part : (k + 1) * part].astype(F32)
                for c in range(n_ctx)
            ]
            tail = []
            for h in range(part // cut):
                at = (t * pieces + k * (part // cut) + h) * group
                tail.append(extra[at : at + group])
            rows.append(jnp.concatenate(tail, 1))
            start = (k * n_tp + t) * part
            out_ref[:, start : start + part] = jnp.concatenate(rows, 0).astype(BF16)


def arrange(recv, part, n_ctx, n_tp):
    return call(
        lambda *refs: arrange_kernel(*refs, n_ctx=n_ctx, n_tp=n_tp),
        "arrange",
        struct((n_ctx * HALF, 2 * part * n_tp), BF16),
        vmem=16 << 20,
    )(recv)


def ship_kernel(sum_ref, out_ref, n_ctx, n_tp):
    part = out_ref.shape[2] - LANES
    width = part * n_tp
    router = sum_ref[:, width:].astype(F32)
    for t in range(n_tp):
        value = sum_ref[:, t * part : (t + 1) * part].astype(F32)
        for c in range(n_ctx):
            main = slice(c * MAIN, (c + 1) * MAIN)
            rest = slice(n_ctx * MAIN + c * REST, n_ctx * MAIN + (c + 1) * REST)
            both = jnp.concatenate([value[main], value[rest]], 0)
            out_ref[c * n_tp + t, :, :part] = both.astype(BF16)
            both = jnp.concatenate([router[main], router[rest]], 0)
            out_ref[c * n_tp + t, :, part:] = both.astype(BF16)


def ship(summed, n_ctx, n_tp):
    part = (summed.shape[1] - LANES) // n_tp
    return call(
        lambda *refs: ship_kernel(*refs, n_ctx=n_ctx, n_tp=n_tp),
        "ship",
        struct((n_ctx * n_tp, HALF, part + LANES), BF16),
        vmem=16 << 20,
    )(summed)


def home_kernel(land_ref, place_ref, logit_ref, input_ref, grad_ref):
    n_dev, _, wide = land_ref.shape
    rows, part = input_ref.shape
    fill = jnp.zeros((PAD - HALF, wide), F32)
    flat = []
    for t in range(n_dev):
        flat += [land_ref[t].astype(F32), fill]
    flat = jnp.concatenate(flat, 0).astype(BF16)
    slot = lax.broadcasted_iota(jnp.int32, (n_dev * PAD, rows), 0)
    pick = (slot == place_ref[...]).astype(BF16)
    home = lax.dot_general(pick, flat[:, :part], OUTER, preferred_element_type=F32)
    input_ref[...] = home.astype(BF16)
    router = lax.dot_general(flat[:, part:], pick, OUTER, preferred_element_type=F32)
    weight = jax.nn.sigmoid(logit_ref[...]).astype(BF16).astype(F32)
    grad_ref[...] = (router[:1] * (1.0 - weight)).astype(BF16)


def take_home(landed, place, logit):
    rows = place.shape[1]
    part = landed.shape[2] - LANES
    return call(
        home_kernel,
        "take_home",
        [struct((rows, part), BF16), struct((1, rows), BF16)],
        vmem=16 << 20,
    )(landed, place, logit)


def join(parts, axis):
    return jnp.concatenate([p[...] for p in parts], axis)


def gate_up_kernel(both_ref, *refs):
    weights = refs[:8]
    here_ref, there_ref, gate_ref, up_ref, x_v, w_v, sem = refs[8:]
    width = x_v.shape[1]
    groups = []
    for k in range(CHUNKS):
        size = width // CHUNKS
        part = slice(k * size, (k + 1) * size)
        pairs = [(both_ref.at[:, part], x_v.at[:, part])]
        pairs += [(w.at[part], w_v.at[n, part]) for n, w in enumerate(weights)]
        group = []
        for n, (source, target) in enumerate(pairs):
            group.append(pltpu.make_async_copy(source, target, sem.at[k * 9 + n]))
            group[-1].start()
        groups.append((part, group))
    for k, (part, group) in enumerate(groups):
        for copy in group:
            copy.wait()
        x = x_v[:, part]
        for first, out in ((0, gate_ref), (4, up_ref)):
            w = jnp.concatenate([w_v[first + n, part] for n in range(4)], 1)
            some = jnp.dot(x, w, preferred_element_type=F32)
            out[...] = some if k == 0 else out[...] + some
    half = here_ref.shape[1]
    for n, out in enumerate((here_ref, there_ref)):
        cols = slice(n * half, (n + 1) * half)
        gate = gate_ref[:, cols]
        out[...] = (gate * jax.nn.sigmoid(gate) * up_ref[:, cols]).astype(BF16)


def gate_up_part(both, sets):
    rows, wide = both.shape
    width = wide // 2
    unit = sets[0][0].shape[1]
    near = pl.BlockSpec(memory_space=pltpu.VMEM)
    return call(
        gate_up_kernel,
        "gate_up_part",
        [struct((rows, 2 * unit), BF16)] * 2 + [struct((rows, 4 * unit), F32)] * 2,
        in_specs=[pl.BlockSpec(memory_space=pl.ANY)] * 9,
        out_specs=[near] * 4,
        scratch_shapes=[
            pltpu.VMEM((rows, width), BF16),
            pltpu.VMEM((8, width, unit), BF16),
            pltpu.SemaphoreType.DMA((9 * CHUNKS,)),
        ],
    )(both, *[s[0] for s in sets], *[s[1] for s in sets])


def back_kernel(n_down, *refs):
    both_ref, gate_ref, up_ref = refs[:3]
    downs, weights = refs[3 : 3 + n_down], refs[3 + n_down : 11 + n_down]
    part_ref, here_ref, there_ref = refs[11 + n_down : 14 + n_down]
    dy_v, down_v, gate_v, up_v, w_v, out_v, in_sem, out_sem = refs[14 + n_down :]
    rows, width = dy_v.shape
    unit = gate_v.shape[1] // 4
    count = [0]

    def load(source, target):
        copy = pltpu.make_async_copy(source, target, in_sem.at[count[0]])
        copy.start()
        count[0] += 1
        return copy

    first = []
    for k in range(2):
        size = width // 2
        cols = slice(k * size, (k + 1) * size)
        group = [load(both_ref.at[:, pl.ds(width + k * size, size)], dy_v.at[:, cols])]
        at = 0
        for w in downs:
            group.append(load(w.at[:, cols], down_v.at[at : at + w.shape[0], cols]))
            at += w.shape[0]
        first.append((cols, group))
    middle = [load(gate_ref, gate_v), load(up_ref, up_v)]
    last = []
    for k in range(4):
        size = width // 4
        cols = slice(k * size, (k + 1) * size)
        last.append((cols, [load(w.at[cols], w_v.at[n, cols]) for n, w in enumerate(weights)]))
    back = None
    for cols, group in first:
        for copy in group:
            copy.wait()
        some = lax.dot_general(dy_v[:, cols], down_v[:, cols], INNER, preferred_element_type=F32)
        back = some if back is None else back + some
    for copy in middle:
        copy.wait()
    total = jnp.zeros((rows, 1), F32)
    for n in range(4):
        cols = slice(n * unit, (n + 1) * unit)
        gate = gate_v[:, cols]
        up = up_v[:, cols]
        value = back[:, cols]
        sig = jax.nn.sigmoid(gate)
        act = gate * sig
        out = here_ref if n < 2 else there_ref
        base = (n % 2) * 2 * unit
        d_gate = value * up * sig * (1.0 + gate * (1.0 - sig))
        out[:, base : base + unit] = d_gate.astype(BF16)
        out[:, base + unit : base + 2 * unit] = (value * act).astype(BF16)
        total = total + jnp.sum(act * up * value, axis=1, keepdims=True)
    out_v[:, width:] = jnp.broadcast_to(total, (rows, LANES)).astype(BF16)
    d = jnp.concatenate([here_ref[...], there_ref[...]], 1)
    sent = []

    def store(cols, k):
        copy = pltpu.make_async_copy(out_v.at[:, cols], part_ref.at[:, cols], out_sem.at[k])
        copy.start()
        sent.append(copy)

    store(slice(width, width + LANES), 4)
    for k, (cols, group) in enumerate(last):
        for copy in group:
            copy.wait()
        w = jnp.concatenate([w_v[n, cols] for n in range(8)], 1)
        out_v[:, cols] = lax.dot_general(d, w, INNER, preferred_element_type=F32).astype(BF16)
        store(cols, k)
    for copy in sent:
        copy.wait()


def back_part(both, gate, up, downs, sets):
    rows, wide = both.shape
    width = wide // 2
    unit = gate.shape[1] // 4
    weights = [w for s in sets for w in s]
    operands = [both, gate, up, *downs, *weights]
    anywhere = pl.BlockSpec(memory_space=pl.ANY)
    near = pl.BlockSpec(memory_space=pltpu.VMEM)
    return call(
        lambda *refs: back_kernel(len(downs), *refs),
        "back_part",
        [struct((rows, width + LANES), BF16)] + [struct((rows, 4 * unit), BF16)] * 2,
        in_specs=[anywhere] * len(operands),
        out_specs=[anywhere, near, near],
        scratch_shapes=[
            pltpu.VMEM((rows, width), BF16),
            pltpu.VMEM((4 * unit, width), BF16),
            pltpu.VMEM((rows, 4 * unit), F32),
            pltpu.VMEM((rows, 4 * unit), F32),
            pltpu.VMEM((8, width, unit), BF16),
            pltpu.VMEM((rows, width + LANES), BF16),
            pltpu.SemaphoreType.DMA((2 * (1 + len(downs)) + 2 + 32,)),
            pltpu.SemaphoreType.DMA((5,)),
        ],
    )(*operands)


def tall_kernel(n_part, *refs):
    gate_ref, up_ref = refs[-2:]
    extra = refs[2 * n_part : -2]
    unit = gate_ref.shape[1]
    x = join(refs[:n_part], 0)
    d = join(refs[n_part : 2 * n_part], 0)
    out = lax.dot_general(x, d, OUTER, preferred_element_type=F32)
    gate, up = out[:, :unit], out[:, unit:]
    if extra:
        gate = gate + extra[0][...].astype(F32)
        up = up + extra[1][...].astype(F32)
    gate_ref[...] = gate.astype(BF16)
    up_ref[...] = up.astype(BF16)


def tall_part(xs, ds, unit, start, steps, rows, addends=(), into=(), flops=0):
    n = len(xs) + len(ds) + len(addends)
    full = rows > steps * PIECE
    return call(
        lambda *refs: tall_kernel(len(xs), *refs[:n], *refs[-2:]),
        "tall_part",
        [struct((rows, unit), BF16)] * 2,
        grid=(steps,),
        in_specs=[
            pl.BlockSpec(
                (x.shape[0], PIECE), lambda i, far=x.shape[1] == FAR * PIECE: (0, i if far else start + i)
            )
            for x in xs
        ]
        + [pl.BlockSpec((d.shape[0], 2 * unit), lambda i, at=at: (0, at)) for d, at in ds]
        + [pl.BlockSpec((PIECE, unit), lambda i: (i, 0))] * len(addends)
        + [pl.BlockSpec(memory_space=pl.ANY)] * len(into),
        out_specs=[pl.BlockSpec((PIECE, unit), lambda i: (start + i if full else i, 0))] * 2,
        input_output_aliases={n + k: k for k in range(len(into))},
        flops=flops,
    )(*xs, *[d for d, _ in ds], *addends, *into)


def flat_kernel(y0, y1, s0, s1, *rest):
    down_ref = rest[-1]
    y = jnp.concatenate([y0[...], y1[...]], 0)
    s = jnp.concatenate([s0[...], s1[...]], 0)
    out = lax.dot_general(s, y, OUTER, preferred_element_type=F32)
    if len(rest) > 1:
        out = out + rest[0][...].astype(F32)
    down_ref[...] = out.astype(BF16)


def flat_part(both, s, which, addend=None, flops=0):
    rows, wide = both[0].shape
    width = wide // 2
    unit = s[0].shape[1] // 2
    steps = width // BLOCK
    y_spec = pl.BlockSpec((rows, BLOCK), lambda i: (0, i + steps))
    s_spec = pl.BlockSpec((rows, unit), lambda i: (0, which))
    o_spec = pl.BlockSpec((unit, BLOCK), lambda i: (0, i))
    extra = () if addend is None else (addend,)
    return call(
        flat_kernel,
        "flat_part",
        struct((unit, width), BF16),
        grid=(steps,),
        in_specs=[y_spec] * 2 + [s_spec] * 2 + [o_spec] * len(extra),
        out_specs=o_spec,
        flops=flops,
    )(*both, *s, *extra)


def flip(value, axis):
    count = lax.axis_size(axis)
    return lax.ppermute(value, axis, [(i, i ^ 1) for i in range(count)])


def after(value, first):
    return lax.optimization_barrier((value, first))[0]


def body(tokens_in, grad_out, router_logit, expert_index, gate_half, up_half, down_half):
    n_ctx = lax.axis_size("ctx")
    n_tp = lax.axis_size("tp")
    logit = router_logit[None]
    route = expert_index.reshape(1, -1)
    send, place = spread(tokens_in, grad_out, logit, route, n_ctx * n_tp)
    recv = lax.all_to_all(send, ("ctx", "tp"), split_axis=0, concat_axis=0, tiled=True)
    mine = arrange(recv, tokens_in.shape[1], n_ctx, n_tp)
    own = (gate_half[0], up_half[0], down_half[0])
    cut = 3 * PAD
    far_mine = flip(mine[:, : FAR * PIECE], "tp")
    gate, down = after((own[0], own[2]), recv)
    up, first, second = lax.optimization_barrier((own[1], down[:cut], down[cut:]))
    gate, far_mine = lax.optimization_barrier((gate, far_mine))
    across = lambda group: tuple(flip(w, "core") for w in group)
    other = (flip(gate, "tp"), flip(up, "tp"))
    own_there = across(own)
    gate_there = flip(other[0], "core")
    first, own_there, gate_there = lax.optimization_barrier((first, own_there, gate_there))
    most, late = flip(first, "tp"), flip(second, "tp")
    sets = (own[:2], other, own_there[:2], (gate_there, flip(other[1], "core")))
    here = lax.all_gather(mine, "z", axis=0, tiled=True)
    here, sets, most = lax.optimization_barrier((here, sets, most))
    beside = flip(here, "core")
    both = (here, beside)
    s_here, s_there, gate, up = gate_up_part(here, sets)
    s = (s_here, flip(s_there, "core"))
    give_down = flat_part(both, s, 1)
    got_down = flip(give_down, "tp")
    most = after(most, s_here)
    late = after(late, give_down)
    downs = (own[2], most, late, own_there[2], flip(most, "core"), flip(late, "core"))
    part, d_here, d_there = back_part(after(here, give_down), gate, up, downs, sets)
    far = lax.all_gather(far_mine, "z", axis=0, tiled=True)
    part, far = lax.optimization_barrier((part, far))
    summed = lax.optimization_barrier(
        lax.psum_scatter(part, "z", scatter_dimension=0, tiled=True)
    )
    far_beside = flip(far, "core")
    d = after((d_here, flip(d_there, "core")), part)
    width, unit = own[0].shape
    steps = width // PIECE - FAR
    give = tall_part(both, [(w, 1) for w in d], unit, FAR, steps, steps * PIECE)
    got = (flip(give[0], "tp"), flip(give[1], "tp"))
    far_d = flip(jnp.concatenate([w[:, 2 * unit :] for w in d], 0), "tp")
    s, d, got_down = lax.optimization_barrier((s, after(d, give[0]), got_down))
    down_grad = flat_part(both, s, 0, got_down, SHORT)
    d, far_d = after((d, far_d), down_grad)
    around = both + (far, far_beside)
    d_all = [(w, 0) for w in (*d, *jnp.split(far_d, 2))]
    top = tall_part(around, d_all, unit, 0, FAR, width, flops=SHORT)
    tall_grads = tall_part(both, d_all[:2], unit, FAR, steps, width, got, top)
    summed = after(summed, top[0])
    shipped = ship(summed, n_ctx, n_tp)
    landed = lax.all_to_all(shipped, ("ctx", "tp"), split_axis=0, concat_axis=0, tiled=True)
    input_grad, logit_grad = take_home(landed, place, logit)
    return input_grad, logit_grad[0], tall_grads[0][None], tall_grads[1][None], down_grad[None]


def solution(mesh):
    n_dp = mesh.shape["dp"]
    fine = Mesh(
        mesh.devices.reshape(n_dp // 2, 2, mesh.shape["ctx"], mesh.shape["tp"]),
        ("z", "core", "ctx", "tp"),
    )
    dp = ("z", "core")
    token = dp + ("ctx",)
    in_specs = (
        P(token, "tp"),
        P(token, "tp"),
        P(token),
        P(token, None),
        P(("ctx", "tp"), None, dp),
        P(("ctx", "tp"), None, dp),
        P(("ctx", "tp"), dp, None),
    )
    out_specs = (
        P(token, "tp"),
        P(token),
        P(("ctx", "tp"), None, dp),
        P(("ctx", "tp"), None, dp),
        P(("ctx", "tp"), dp, None),
    )
    return jax.shard_map(body, mesh=fine, in_specs=in_specs, out_specs=out_specs, check_vma=False)
```

```python
import jax
import jax.numpy as jnp
from jax import lax
from jax.experimental import pallas as pl
from jax.experimental.pallas import tpu as pltpu
from jax.sharding import Mesh, PartitionSpec as P

HALF = 10
MAIN = 8
REST = HALF - MAIN
PAD = 16
LANES = 128
BLOCK = 2560
PIECE = 640
FAR = 3
CHUNKS = 4
SHORT = 34_590_000_000
INNER = (((1,), (1,)), ((), ()))
OUTER = (((0,), (0,)), ((), ()))
F32 = jnp.float32
BF16 = jnp.bfloat16


def call(kernel, name, out_shape, vmem=60 << 20, flops=0, **kw):
    return pl.pallas_call(
        kernel,
        out_shape=out_shape,
        compiler_params=pltpu.CompilerParams(vmem_limit_bytes=vmem),
        cost_estimate=pl.CostEstimate(flops=flops, bytes_accessed=0, transcendentals=0),
        name=name,
        **kw,
    )


def struct(shape, dtype):
    return jax.ShapeDtypeStruct(shape, dtype)


def whole(shape):
    return pl.BlockSpec(shape, lambda i: (0,) * len(shape))


def spread_kernel(x_ref, dy_ref, logit_ref, route_ref, send_ref, place_ref, n_dev):
    rows, part = x_ref.shape
    route = route_ref[...]
    expert = lax.broadcasted_iota(jnp.int32, (n_dev // 2, rows), 0)
    hit = (route == expert).astype(F32)
    row = lax.broadcasted_iota(jnp.int32, (rows, rows), 0)
    col = lax.broadcasted_iota(jnp.int32, (rows, rows), 1)
    earlier = (row < col).astype(BF16)
    before = jnp.dot(hit.astype(BF16), earlier, preferred_element_type=F32)
    rank = jnp.sum(before * hit, axis=0, keepdims=True).astype(jnp.int32)
    member = (rank >= HALF).astype(jnp.int32)
    place = (2 * route + member) * PAD + rank - HALF * member
    place_ref[...] = place
    weight = jax.nn.sigmoid(logit_ref[...]).astype(BF16).astype(F32)
    slot = lax.broadcasted_iota(jnp.int32, (n_dev * MAIN, rows), 0)
    target, r = slot // MAIN, slot % MAIN
    pieces = MAIN // REST
    main = (target * PAD + r == place).astype(F32)
    rest = (target * PAD + MAIN + r // pieces == place).astype(F32)
    which = (slot % pieces)[:, :1]
    cut = 2 * part // pieces
    extra = jnp.zeros((n_dev * MAIN, cut), F32)
    for k, (scale, value) in enumerate(((1.0, x_ref[...]), (weight, dy_ref[...]))):
        out = jnp.dot((main * scale).astype(BF16), value, preferred_element_type=F32)
        out = out.astype(BF16)
        for t in range(n_dev):
            send_ref[t, :, k * part : (k + 1) * part] = out[t * MAIN : (t + 1) * MAIN]
        tail = jnp.dot((rest * scale).astype(BF16), value, preferred_element_type=F32)
        for h in range(part // cut):
            chosen = which == k * (part // cut) + h
            extra = jnp.where(chosen, tail[:, h * cut : (h + 1) * cut], extra)
    extra = extra.astype(BF16)
    for t in range(n_dev):
        send_ref[t, :, 2 * part :] = extra[t * MAIN : (t + 1) * MAIN]


def spread(x, dy, logit, route, n_dev):
    rows, part = x.shape
    wide = 2 * part * HALF // MAIN
    return call(
        lambda *refs: spread_kernel(*refs, n_dev=n_dev),
        "spread",
        [struct((n_dev, MAIN, wide), BF16), struct((1, rows), jnp.int32)],
    )(x, dy, logit, route)


def arrange_kernel(recv_ref, out_ref, n_ctx, n_tp):
    n_dev = n_ctx * n_tp
    part = out_ref.shape[1] // (2 * n_tp)
    pieces = MAIN // REST
    cut = 2 * part // pieces
    extra = jnp.concatenate([recv_ref[t, :, 2 * part :] for t in range(n_dev)], 0)
    size = n_dev * MAIN
    row = lax.broadcasted_iota(jnp.int32, (size, size), 0)
    col = lax.broadcasted_iota(jnp.int32, (size, size), 1)
    group = n_ctx * REST
    t, p = row // (pieces * group), row // group % pieces
    c, i = row // REST % n_ctx, row % REST
    order = (col == (c * n_tp + t) * MAIN + i * pieces + p).astype(BF16)
    extra = jnp.dot(order, extra, preferred_element_type=F32)
    for k in range(2):
        for t in range(n_tp):
            rows = [
                recv_ref[c * n_tp + t, :, k * part : (k + 1) * part].astype(F32)
                for c in range(n_ctx)
            ]
            tail = []
            for h in range(part // cut):
                at = (t * pieces + k * (part // cut) + h) * group
                tail.append(extra[at : at + group])
            rows.append(jnp.concatenate(tail, 1))
            start = (k * n_tp + t) * part
            out_ref[:, start : start + part] = jnp.concatenate(rows, 0).astype(BF16)


def arrange(recv, part, n_ctx, n_tp):
    return call(
        lambda *refs: arrange_kernel(*refs, n_ctx=n_ctx, n_tp=n_tp),
        "arrange",
        struct((n_ctx * HALF, 2 * part * n_tp), BF16),
        vmem=16 << 20,
    )(recv)


def ship_kernel(sum_ref, out_ref, n_ctx, n_tp):
    width = sum_ref.shape[1] - LANES
    part = width // n_tp
    pieces = MAIN // REST
    cut = out_ref.shape[2] - part - LANES
    group = n_ctx * REST
    row = lax.broadcasted_iota(jnp.int32, (pieces * group, pieces * group), 0)
    col = lax.broadcasted_iota(jnp.int32, (pieces * group, pieces * group), 1)
    order = (col == row % pieces * group + row // pieces).astype(BF16)
    router = sum_ref[:, width:]
    fill = jnp.zeros((group, pieces * cut - part - LANES), BF16)
    for t in range(n_tp):
        value = sum_ref[:, t * part : (t + 1) * part]
        rest = jnp.concatenate([value[-group:], router[-group:], fill], 1).astype(F32)
        rest = [rest[:, p * cut : (p + 1) * cut] for p in range(pieces)]
        rest = jnp.concatenate(rest, 0).astype(BF16)
        rest = jnp.dot(order, rest, preferred_element_type=F32).astype(BF16)
        for c in range(n_ctx):
            main = slice(c * MAIN, (c + 1) * MAIN)
            out_ref[c * n_tp + t, :, :part] = value[main]
            out_ref[c * n_tp + t, :, part : part + cut] = rest[main]
            out_ref[c * n_tp + t, :, part + cut :] = router[main]


def ship(summed, n_ctx, n_tp):
    part = (summed.shape[1] - LANES) // n_tp
    pieces = MAIN // REST
    cut = -(-(part + LANES) // (pieces * LANES)) * LANES
    return call(
        lambda *refs: ship_kernel(*refs, n_ctx=n_ctx, n_tp=n_tp),
        "ship",
        struct((n_ctx * n_tp, MAIN, part + cut + LANES), BF16),
        vmem=16 << 20,
    )(summed)


def home_kernel(land_ref, place_ref, logit_ref, input_ref, grad_ref):
    n_dev, _, wide = land_ref.shape
    rows, part = input_ref.shape
    pieces = MAIN // REST
    cut = wide - part - LANES
    flat = jnp.concatenate([land_ref[t].astype(F32) for t in range(n_dev)], 0).astype(BF16)
    slot = lax.broadcasted_iota(jnp.int32, (n_dev * MAIN, rows), 0)
    target, r = slot // MAIN, slot % MAIN
    place = place_ref[...]
    take = lambda chosen, value: lax.dot_general(
        chosen, value, OUTER, preferred_element_type=F32
    )
    main = (target * PAD + r == place).astype(BF16)
    rest_row = target * PAD + MAIN + r // pieces == place
    tail = flat[:, part : part + cut]
    rest = []
    for p in range(pieces):
        chosen = (rest_row & (r % pieces == p)).astype(BF16)
        rest.append(take(chosen, tail))
    rest = jnp.concatenate(rest, 1)
    input_ref[...] = (take(main, flat[:, :part]) + rest[:, :part]).astype(BF16)
    first = part % cut
    router = take(flat[:, part + cut :], main) + take(tail[:, first : first + LANES], chosen)
    weight = jax.nn.sigmoid(logit_ref[...]).astype(BF16).astype(F32)
    grad_ref[...] = (router[:1] * (1.0 - weight)).astype(BF16)


def take_home(landed, place, logit, part):
    rows = place.shape[1]
    return call(
        home_kernel,
        "take_home",
        [struct((rows, part), BF16), struct((1, rows), BF16)],
        vmem=16 << 20,
    )(landed, place, logit)


def join(parts, axis):
    return jnp.concatenate([p[...] for p in parts], axis)


def gate_up_kernel(both_ref, *refs):
    weights = refs[:8]
    here_ref, there_ref, gate_ref, up_ref, x_v, w_v, sem = refs[8:]
    width = x_v.shape[1]
    groups = []
    for k in range(CHUNKS):
        size = width // CHUNKS
        part = slice(k * size, (k + 1) * size)
        pairs = [(both_ref.at[:, part], x_v.at[:, part])]
        pairs += [(w.at[part], w_v.at[n, part]) for n, w in enumerate(weights)]
        group = []
        for n, (source, target) in enumerate(pairs):
            group.append(pltpu.make_async_copy(source, target, sem.at[k * 9 + n]))
            group[-1].start()
        groups.append((part, group))
    for k, (part, group) in enumerate(groups):
        for copy in group:
            copy.wait()
        x = x_v[:, part]
        for first, out in ((0, gate_ref), (4, up_ref)):
            w = jnp.concatenate([w_v[first + n, part] for n in range(4)], 1)
            some = jnp.dot(x, w, preferred_element_type=F32)
            out[...] = some if k == 0 else out[...] + some
    half = here_ref.shape[1]
    for n, out in enumerate((here_ref, there_ref)):
        cols = slice(n * half, (n + 1) * half)
        gate = gate_ref[:, cols]
        out[...] = (gate * jax.nn.sigmoid(gate) * up_ref[:, cols]).astype(BF16)


def gate_up_part(both, sets):
    rows, wide = both.shape
    width = wide // 2
    unit = sets[0][0].shape[1]
    near = pl.BlockSpec(memory_space=pltpu.VMEM)
    return call(
        gate_up_kernel,
        "gate_up_part",
        [struct((rows, 2 * unit), BF16)] * 2 + [struct((rows, 4 * unit), F32)] * 2,
        in_specs=[pl.BlockSpec(memory_space=pl.ANY)] * 9,
        out_specs=[near] * 4,
        scratch_shapes=[
            pltpu.VMEM((rows, width), BF16),
            pltpu.VMEM((8, width, unit), BF16),
            pltpu.SemaphoreType.DMA((9 * CHUNKS,)),
        ],
    )(both, *[s[0] for s in sets], *[s[1] for s in sets])


def back_kernel(n_down, *refs):
    both_ref, gate_ref, up_ref = refs[:3]
    downs, weights = refs[3 : 3 + n_down], refs[3 + n_down : 11 + n_down]
    part_ref, here_ref, there_ref = refs[11 + n_down : 14 + n_down]
    dy_v, down_v, gate_v, up_v, w_v, out_v, in_sem, out_sem = refs[14 + n_down :]
    rows, width = dy_v.shape
    unit = gate_v.shape[1] // 4
    count = [0]

    def load(source, target):
        copy = pltpu.make_async_copy(source, target, in_sem.at[count[0]])
        copy.start()
        count[0] += 1
        return copy

    first = []
    for k in range(2):
        size = width // 2
        cols = slice(k * size, (k + 1) * size)
        group = [load(both_ref.at[:, pl.ds(width + k * size, size)], dy_v.at[:, cols])]
        at = 0
        for w in downs:
            group.append(load(w.at[:, cols], down_v.at[at : at + w.shape[0], cols]))
            at += w.shape[0]
        first.append((cols, group))
    middle = [load(gate_ref, gate_v), load(up_ref, up_v)]
    last = []
    for k in range(4):
        size = width // 4
        cols = slice(k * size, (k + 1) * size)
        last.append((cols, [load(w.at[cols], w_v.at[n, cols]) for n, w in enumerate(weights)]))
    back = None
    for cols, group in first:
        for copy in group:
            copy.wait()
        some = lax.dot_general(dy_v[:, cols], down_v[:, cols], INNER, preferred_element_type=F32)
        back = some if back is None else back + some
    for copy in middle:
        copy.wait()
    total = jnp.zeros((rows, 1), F32)
    for n in range(4):
        cols = slice(n * unit, (n + 1) * unit)
        gate = gate_v[:, cols]
        up = up_v[:, cols]
        value = back[:, cols]
        sig = jax.nn.sigmoid(gate)
        act = gate * sig
        out = here_ref if n < 2 else there_ref
        base = (n % 2) * 2 * unit
        d_gate = value * up * sig * (1.0 + gate * (1.0 - sig))
        out[:, base : base + unit] = d_gate.astype(BF16)
        out[:, base + unit : base + 2 * unit] = (value * act).astype(BF16)
        total = total + jnp.sum(act * up * value, axis=1, keepdims=True)
    out_v[:, width:] = jnp.broadcast_to(total, (rows, LANES)).astype(BF16)
    d = jnp.concatenate([here_ref[...], there_ref[...]], 1)
    sent = []

    def store(cols, k):
        copy = pltpu.make_async_copy(out_v.at[:, cols], part_ref.at[:, cols], out_sem.at[k])
        copy.start()
        sent.append(copy)

    store(slice(width, width + LANES), 4)
    for k, (cols, group) in enumerate(last):
        for copy in group:
            copy.wait()
        w = jnp.concatenate([w_v[n, cols] for n in range(8)], 1)
        out_v[:, cols] = lax.dot_general(d, w, INNER, preferred_element_type=F32).astype(BF16)
        store(cols, k)
    for copy in sent:
        copy.wait()


def back_part(both, gate, up, downs, sets):
    rows, wide = both.shape
    width = wide // 2
    unit = gate.shape[1] // 4
    weights = [w for s in sets for w in s]
    operands = [both, gate, up, *downs, *weights]
    anywhere = pl.BlockSpec(memory_space=pl.ANY)
    near = pl.BlockSpec(memory_space=pltpu.VMEM)
    return call(
        lambda *refs: back_kernel(len(downs), *refs),
        "back_part",
        [struct((rows, width + LANES), BF16)] + [struct((rows, 4 * unit), BF16)] * 2,
        in_specs=[anywhere] * len(operands),
        out_specs=[anywhere, near, near],
        scratch_shapes=[
            pltpu.VMEM((rows, width), BF16),
            pltpu.VMEM((4 * unit, width), BF16),
            pltpu.VMEM((rows, 4 * unit), F32),
            pltpu.VMEM((rows, 4 * unit), F32),
            pltpu.VMEM((8, width, unit), BF16),
            pltpu.VMEM((rows, width + LANES), BF16),
            pltpu.SemaphoreType.DMA((2 * (1 + len(downs)) + 2 + 32,)),
            pltpu.SemaphoreType.DMA((5,)),
        ],
    )(*operands)


def tall_kernel(n_part, *refs):
    gate_ref, up_ref = refs[-2:]
    extra = refs[2 * n_part : -2]
    unit = gate_ref.shape[1]
    x = join(refs[:n_part], 0)
    d = join(refs[n_part : 2 * n_part], 0)
    out = lax.dot_general(x, d, OUTER, preferred_element_type=F32)
    gate, up = out[:, :unit], out[:, unit:]
    if extra:
        gate = gate + extra[0][...].astype(F32)
        up = up + extra[1][...].astype(F32)
    gate_ref[...] = gate.astype(BF16)
    up_ref[...] = up.astype(BF16)


def tall_part(xs, ds, unit, start, steps, rows, addends=(), into=(), flops=0):
    n = len(xs) + len(ds) + len(addends)
    full = rows > steps * PIECE
    return call(
        lambda *refs: tall_kernel(len(xs), *refs[:n], *refs[-2:]),
        "tall_part",
        [struct((rows, unit), BF16)] * 2,
        grid=(steps,),
        in_specs=[
            pl.BlockSpec(
                (x.shape[0], PIECE), lambda i, far=x.shape[1] == FAR * PIECE: (0, i if far else start + i)
            )
            for x in xs
        ]
        + [pl.BlockSpec((d.shape[0], 2 * unit), lambda i, at=at: (0, at)) for d, at in ds]
        + [pl.BlockSpec((PIECE, unit), lambda i: (i, 0))] * len(addends)
        + [pl.BlockSpec(memory_space=pl.ANY)] * len(into),
        out_specs=[pl.BlockSpec((PIECE, unit), lambda i: (start + i if full else i, 0))] * 2,
        input_output_aliases={n + k: k for k in range(len(into))},
        flops=flops,
    )(*xs, *[d for d, _ in ds], *addends, *into)


def flat_kernel(y0, y1, s0, s1, *rest):
    down_ref = rest[-1]
    y = jnp.concatenate([y0[...], y1[...]], 0)
    s = jnp.concatenate([s0[...], s1[...]], 0)
    out = lax.dot_general(s, y, OUTER, preferred_element_type=F32)
    if len(rest) > 1:
        out = out + rest[0][...].astype(F32)
    down_ref[...] = out.astype(BF16)


def flat_part(both, s, which, addend=None, flops=0):
    rows, wide = both[0].shape
    width = wide // 2
    unit = s[0].shape[1] // 2
    steps = width // BLOCK
    y_spec = pl.BlockSpec((rows, BLOCK), lambda i: (0, i + steps))
    s_spec = pl.BlockSpec((rows, unit), lambda i: (0, which))
    o_spec = pl.BlockSpec((unit, BLOCK), lambda i: (0, i))
    extra = () if addend is None else (addend,)
    return call(
        flat_kernel,
        "flat_part",
        struct((unit, width), BF16),
        grid=(steps,),
        in_specs=[y_spec] * 2 + [s_spec] * 2 + [o_spec] * len(extra),
        out_specs=o_spec,
        flops=flops,
    )(*both, *s, *extra)


def flip(value, axis):
    count = lax.axis_size(axis)
    return lax.ppermute(value, axis, [(i, i ^ 1) for i in range(count)])


def after(value, first):
    return lax.optimization_barrier((value, first))[0]


def body(tokens_in, grad_out, router_logit, expert_index, gate_half, up_half, down_half):
    n_ctx = lax.axis_size("ctx")
    n_tp = lax.axis_size("tp")
    logit = router_logit[None]
    route = expert_index.reshape(1, -1)
    send, place = spread(tokens_in, grad_out, logit, route, n_ctx * n_tp)
    recv = lax.all_to_all(send, ("ctx", "tp"), split_axis=0, concat_axis=0, tiled=True)
    mine = arrange(recv, tokens_in.shape[1], n_ctx, n_tp)
    own = (gate_half[0], up_half[0], down_half[0])
    cut = 3 * PAD
    far_mine = flip(mine[:, : FAR * PIECE], "tp")
    gate, down = after((own[0], own[2]), recv)
    up, first, second = lax.optimization_barrier((own[1], down[:cut], down[cut:]))
    gate, far_mine = lax.optimization_barrier((gate, far_mine))
    across = lambda group: tuple(flip(w, "core") for w in group)
    other = (flip(gate, "tp"), flip(up, "tp"))
    own_there = across(own)
    gate_there = flip(other[0], "core")
    first, own_there, gate_there = lax.optimization_barrier((first, own_there, gate_there))
    most, late = flip(first, "tp"), flip(second, "tp")
    sets = (own[:2], other, own_there[:2], (gate_there, flip(other[1], "core")))
    here = lax.all_gather(mine, "z", axis=0, tiled=True)
    here, sets, most = lax.optimization_barrier((here, sets, most))
    beside = flip(here, "core")
    both = (here, beside)
    s_here, s_there, gate, up = gate_up_part(here, sets)
    s = (s_here, flip(s_there, "core"))
    give_down = flat_part(both, s, 1)
    got_down = flip(give_down, "tp")
    most = after(most, s_here)
    late = after(late, give_down)
    downs = (own[2], most, late, own_there[2], flip(most, "core"), flip(late, "core"))
    part, d_here, d_there = back_part(after(here, give_down), gate, up, downs, sets)
    far = lax.all_gather(far_mine, "z", axis=0, tiled=True)
    part, far = lax.optimization_barrier((part, far))
    summed = lax.optimization_barrier(
        lax.psum_scatter(part, "z", scatter_dimension=0, tiled=True)
    )
    far_beside = flip(far, "core")
    d = after((d_here, flip(d_there, "core")), part)
    width, unit = own[0].shape
    steps = width // PIECE - FAR
    give = tall_part(both, [(w, 1) for w in d], unit, FAR, steps, steps * PIECE)
    got = (flip(give[0], "tp"), flip(give[1], "tp"))
    far_d = flip(jnp.concatenate([w[:, 2 * unit :] for w in d], 0), "tp")
    s, d, got_down = lax.optimization_barrier((s, after(d, give[0]), got_down))
    down_grad = flat_part(both, s, 0, got_down, SHORT)
    d, far_d = after((d, far_d), down_grad)
    around = both + (far, far_beside)
    d_all = [(w, 0) for w in (*d, *jnp.split(far_d, 2))]
    top = tall_part(around, d_all, unit, 0, FAR, width, flops=SHORT)
    tall_grads = tall_part(both, d_all[:2], unit, FAR, steps, width, got, top)
    summed = after(summed, top[0])
    shipped = ship(summed, n_ctx, n_tp)
    landed = lax.all_to_all(shipped, ("ctx", "tp"), split_axis=0, concat_axis=0, tiled=True)
    input_grad, logit_grad = take_home(landed, place, logit, tokens_in.shape[1])
    return input_grad, logit_grad[0], tall_grads[0][None], tall_grads[1][None], down_grad[None]


def solution(mesh):
    n_dp = mesh.shape["dp"]
    fine = Mesh(
        mesh.devices.reshape(n_dp // 2, 2, mesh.shape["ctx"], mesh.shape["tp"]),
        ("z", "core", "ctx", "tp"),
    )
    dp = ("z", "core")
    token = dp + ("ctx",)
    in_specs = (
        P(token, "tp"),
        P(token, "tp"),
        P(token),
        P(token, None),
        P(("ctx", "tp"), None, dp),
        P(("ctx", "tp"), None, dp),
        P(("ctx", "tp"), dp, None),
    )
    out_specs = (
        P(token, "tp"),
        P(token),
        P(("ctx", "tp"), None, dp),
        P(("ctx", "tp"), None, dp),
        P(("ctx", "tp"), dp, None),
    )
    return jax.shard_map(body, mesh=fine, in_specs=in_specs, out_specs=out_specs, check_vma=False)
```

```python
import jax
import jax.numpy as jnp
from jax import lax
from jax.experimental import pallas as pl
from jax.experimental.pallas import tpu as pltpu
from jax.sharding import Mesh, PartitionSpec as P

HALF = 10
MAIN = 8
REST = HALF - MAIN
PAD = 16
LANES = 128
BLOCK = 2560
PIECE = 640
FAR = 3
CHUNKS = 4
SHORT = 34_590_000_000
INNER = (((1,), (1,)), ((), ()))
OUTER = (((0,), (0,)), ((), ()))
F32 = jnp.float32
BF16 = jnp.bfloat16


def call(kernel, name, out_shape, vmem=60 << 20, flops=0, **kw):
    return pl.pallas_call(
        kernel,
        out_shape=out_shape,
        compiler_params=pltpu.CompilerParams(vmem_limit_bytes=vmem),
        cost_estimate=pl.CostEstimate(flops=flops, bytes_accessed=0, transcendentals=0),
        name=name,
        **kw,
    )


def struct(shape, dtype):
    return jax.ShapeDtypeStruct(shape, dtype)


def whole(shape):
    return pl.BlockSpec(shape, lambda i: (0,) * len(shape))


def spread_kernel(x_ref, dy_ref, logit_ref, route_ref, send_ref, place_ref, n_dev):
    rows, part = x_ref.shape
    route = route_ref[...]
    expert = lax.broadcasted_iota(jnp.int32, (n_dev // 2, rows), 0)
    hit = (route == expert).astype(F32)
    row = lax.broadcasted_iota(jnp.int32, (rows, rows), 0)
    col = lax.broadcasted_iota(jnp.int32, (rows, rows), 1)
    earlier = (row < col).astype(BF16)
    before = jnp.dot(hit.astype(BF16), earlier, preferred_element_type=F32)
    rank = jnp.sum(before * hit, axis=0, keepdims=True).astype(jnp.int32)
    member = (rank >= HALF).astype(jnp.int32)
    place = (2 * route + member) * PAD + rank - HALF * member
    place_ref[...] = place
    weight = jax.nn.sigmoid(logit_ref[...]).astype(BF16).astype(F32)
    slot = lax.broadcasted_iota(jnp.int32, (n_dev * MAIN, rows), 0)
    target, r = slot // MAIN, slot % MAIN
    pieces = MAIN // REST
    main = (target * PAD + r == place).astype(F32)
    rest = (target * PAD + MAIN + r // pieces == place).astype(F32)
    which = (slot % pieces)[:, :1]
    cut = 2 * part // pieces
    extra = jnp.zeros((n_dev * MAIN, cut), F32)
    for k, (scale, value) in enumerate(((1.0, x_ref[...]), (weight, dy_ref[...]))):
        out = jnp.dot((main * scale).astype(BF16), value, preferred_element_type=F32)
        out = out.astype(BF16)
        for t in range(n_dev):
            send_ref[t, :, k * part : (k + 1) * part] = out[t * MAIN : (t + 1) * MAIN]
        tail = jnp.dot((rest * scale).astype(BF16), value, preferred_element_type=F32)
        for h in range(part // cut):
            chosen = which == k * (part // cut) + h
            extra = jnp.where(chosen, tail[:, h * cut : (h + 1) * cut], extra)
    extra = extra.astype(BF16)
    for t in range(n_dev):
        send_ref[t, :, 2 * part :] = extra[t * MAIN : (t + 1) * MAIN]


def spread(x, dy, logit, route, n_dev):
    rows, part = x.shape
    wide = 2 * part * HALF // MAIN
    return call(
        lambda *refs: spread_kernel(*refs, n_dev=n_dev),
        "spread",
        [struct((n_dev, MAIN, wide), BF16), struct((1, rows), jnp.int32)],
    )(x, dy, logit, route)


def arrange_kernel(recv_ref, out_ref, n_ctx, n_tp):
    n_dev = n_ctx * n_tp
    part = out_ref.shape[1] // (2 * n_tp)
    pieces = MAIN // REST
    cut = 2 * part // pieces
    extra = jnp.concatenate([recv_ref[t, :, 2 * part :] for t in range(n_dev)], 0)
    size = n_dev * MAIN
    row = lax.broadcasted_iota(jnp.int32, (size, size), 0)
    col = lax.broadcasted_iota(jnp.int32, (size, size), 1)
    group = n_ctx * REST
    t, p = row // (pieces * group), row // group % pieces
    c, i = row // REST % n_ctx, row % REST
    order = (col == (c * n_tp + t) * MAIN + i * pieces + p).astype(BF16)
    extra = jnp.dot(order, extra, preferred_element_type=F32)
    for k in range(2):
        for t in range(n_tp):
            rows = [
                recv_ref[c * n_tp + t, :, k * part : (k + 1) * part].astype(F32)
                for c in range(n_ctx)
            ]
            tail = []
            for h in range(part // cut):
                at = (t * pieces + k * (part // cut) + h) * group
                tail.append(extra[at : at + group])
            rows.append(jnp.concatenate(tail, 1))
            start = (k * n_tp + t) * part
            out_ref[:, start : start + part] = jnp.concatenate(rows, 0).astype(BF16)


def arrange(recv, part, n_ctx, n_tp):
    return call(
        lambda *refs: arrange_kernel(*refs, n_ctx=n_ctx, n_tp=n_tp),
        "arrange",
        struct((n_ctx * HALF, 2 * part * n_tp), BF16),
        vmem=16 << 20,
    )(recv)


def ship_kernel(sum_ref, out_ref, n_ctx, n_tp):
    width = sum_ref.shape[1] - LANES
    part = width // n_tp
    pieces = MAIN // REST
    cut = out_ref.shape[2] - part - LANES
    group = n_ctx * REST
    row = lax.broadcasted_iota(jnp.int32, (pieces * group, pieces * group), 0)
    col = lax.broadcasted_iota(jnp.int32, (pieces * group, pieces * group), 1)
    order = (col == row % pieces * group + row // pieces).astype(BF16)
    router = sum_ref[:, width:]
    fill = jnp.zeros((group, pieces * cut - part - LANES), BF16)
    for t in range(n_tp):
        value = sum_ref[:, t * part : (t + 1) * part]
        rest = jnp.concatenate([value[-group:], router[-group:], fill], 1).astype(F32)
        rest = [rest[:, p * cut : (p + 1) * cut] for p in range(pieces)]
        rest = jnp.concatenate(rest, 0).astype(BF16)
        rest = jnp.dot(order, rest, preferred_element_type=F32).astype(BF16)
        for c in range(n_ctx):
            main = slice(c * MAIN, (c + 1) * MAIN)
            out_ref[c * n_tp + t, :, :part] = value[main]
            out_ref[c * n_tp + t, :, part : part + cut] = rest[main]
            out_ref[c * n_tp + t, :, part + cut :] = router[main]


def ship(summed, n_ctx, n_tp):
    part = (summed.shape[1] - LANES) // n_tp
    pieces = MAIN // REST
    cut = -(-(part + LANES) // (pieces * LANES)) * LANES
    return call(
        lambda *refs: ship_kernel(*refs, n_ctx=n_ctx, n_tp=n_tp),
        "ship",
        struct((n_ctx * n_tp, MAIN, part + cut + LANES), BF16),
        vmem=16 << 20,
    )(summed)


def home_kernel(land_ref, place_ref, logit_ref, input_ref, grad_ref):
    n_dev, _, wide = land_ref.shape
    rows, part = input_ref.shape
    pieces = MAIN // REST
    cut = wide - part - LANES
    flat = jnp.concatenate([land_ref[t].astype(F32) for t in range(n_dev)], 0).astype(BF16)
    slot = lax.broadcasted_iota(jnp.int32, (n_dev * MAIN, rows), 0)
    target, r = slot // MAIN, slot % MAIN
    place = place_ref[...]
    take = lambda chosen, value: lax.dot_general(
        chosen, value, OUTER, preferred_element_type=F32
    )
    main = (target * PAD + r == place).astype(BF16)
    rest_row = target * PAD + MAIN + r // pieces == place
    tail = flat[:, part : part + cut]
    rest = []
    for p in range(pieces):
        chosen = (rest_row & (r % pieces == p)).astype(BF16)
        rest.append(take(chosen, tail))
    rest = jnp.concatenate(rest, 1)
    input_ref[...] = (take(main, flat[:, :part]) + rest[:, :part]).astype(BF16)
    first = part % cut
    router = take(flat[:, part + cut :], main) + take(tail[:, first : first + LANES], chosen)
    weight = jax.nn.sigmoid(logit_ref[...]).astype(BF16).astype(F32)
    grad_ref[...] = (router[:1] * (1.0 - weight)).astype(BF16)


def take_home(landed, place, logit, part):
    rows = place.shape[1]
    return call(
        home_kernel,
        "take_home",
        [struct((rows, part), BF16), struct((1, rows), BF16)],
        vmem=16 << 20,
    )(landed, place, logit)


def join(parts, axis):
    return jnp.concatenate([p[...] for p in parts], axis)


def gate_up_kernel(both_ref, *refs):
    weights = refs[:8]
    here_ref, there_ref, gate_ref, up_ref, x_v, w_v, sem = refs[8:]
    width = x_v.shape[1]
    groups = []
    for k in range(CHUNKS):
        size = width // CHUNKS
        part = slice(k * size, (k + 1) * size)
        pairs = [(both_ref.at[:, part], x_v.at[:, part])]
        pairs += [(w.at[part], w_v.at[n, part]) for n, w in enumerate(weights)]
        group = []
        for n, (source, target) in enumerate(pairs):
            group.append(pltpu.make_async_copy(source, target, sem.at[k * 9 + n]))
            group[-1].start()
        groups.append((part, group))
    for k, (part, group) in enumerate(groups):
        for copy in group:
            copy.wait()
        x = x_v[:, part]
        for first, out in ((0, gate_ref), (4, up_ref)):
            w = jnp.concatenate([w_v[first + n, part] for n in range(4)], 1)
            some = jnp.dot(x, w, preferred_element_type=F32)
            out[...] = some if k == 0 else out[...] + some
    half = here_ref.shape[1]
    for n, out in enumerate((here_ref, there_ref)):
        cols = slice(n * half, (n + 1) * half)
        gate = gate_ref[:, cols]
        out[...] = (gate * jax.nn.sigmoid(gate) * up_ref[:, cols]).astype(BF16)


def gate_up_part(both, sets):
    rows, wide = both.shape
    width = wide // 2
    unit = sets[0][0].shape[1]
    near = pl.BlockSpec(memory_space=pltpu.VMEM)
    return call(
        gate_up_kernel,
        "gate_up_part",
        [struct((rows, 2 * unit), BF16)] * 2 + [struct((rows, 4 * unit), F32)] * 2,
        in_specs=[pl.BlockSpec(memory_space=pl.ANY)] * 9,
        out_specs=[near] * 4,
        scratch_shapes=[
            pltpu.VMEM((rows, width), BF16),
            pltpu.VMEM((8, width, unit), BF16),
            pltpu.SemaphoreType.DMA((9 * CHUNKS,)),
        ],
    )(both, *[s[0] for s in sets], *[s[1] for s in sets])


def back_kernel(n_down, *refs):
    both_ref, gate_ref, up_ref = refs[:3]
    downs, weights = refs[3 : 3 + n_down], refs[3 + n_down : 11 + n_down]
    part_ref, here_ref, there_ref = refs[11 + n_down : 14 + n_down]
    dy_v, down_v, gate_v, up_v, w_v, out_v, in_sem, out_sem = refs[14 + n_down :]
    rows, width = dy_v.shape
    unit = gate_v.shape[1] // 4
    count = [0]

    def load(source, target):
        copy = pltpu.make_async_copy(source, target, in_sem.at[count[0]])
        copy.start()
        count[0] += 1
        return copy

    first = []
    for k in range(2):
        size = width // 2
        cols = slice(k * size, (k + 1) * size)
        group = [load(both_ref.at[:, pl.ds(width + k * size, size)], dy_v.at[:, cols])]
        at = 0
        for w in downs:
            group.append(load(w.at[:, cols], down_v.at[at : at + w.shape[0], cols]))
            at += w.shape[0]
        first.append((cols, group))
    middle = [load(gate_ref, gate_v), load(up_ref, up_v)]
    last = []
    for k in range(4):
        size = width // 4
        cols = slice(k * size, (k + 1) * size)
        last.append((cols, [load(w.at[cols], w_v.at[n, cols]) for n, w in enumerate(weights)]))
    back = None
    for cols, group in first:
        for copy in group:
            copy.wait()
        some = lax.dot_general(dy_v[:, cols], down_v[:, cols], INNER, preferred_element_type=F32)
        back = some if back is None else back + some
    for copy in middle:
        copy.wait()
    total = jnp.zeros((rows, 1), F32)
    for n in range(4):
        cols = slice(n * unit, (n + 1) * unit)
        gate = gate_v[:, cols]
        up = up_v[:, cols]
        value = back[:, cols]
        sig = jax.nn.sigmoid(gate)
        act = gate * sig
        out = here_ref if n < 2 else there_ref
        base = (n % 2) * 2 * unit
        d_gate = value * up * sig * (1.0 + gate * (1.0 - sig))
        out[:, base : base + unit] = d_gate.astype(BF16)
        out[:, base + unit : base + 2 * unit] = (value * act).astype(BF16)
        total = total + jnp.sum(act * up * value, axis=1, keepdims=True)
    out_v[:, width:] = jnp.broadcast_to(total, (rows, LANES)).astype(BF16)
    d = jnp.concatenate([here_ref[...], there_ref[...]], 1)
    sent = []

    def store(cols, k):
        copy = pltpu.make_async_copy(out_v.at[:, cols], part_ref.at[:, cols], out_sem.at[k])
        copy.start()
        sent.append(copy)

    store(slice(width, width + LANES), 4)
    for k, (cols, group) in enumerate(last):
        for copy in group:
            copy.wait()
        w = jnp.concatenate([w_v[n, cols] for n in range(8)], 1)
        out_v[:, cols] = lax.dot_general(d, w, INNER, preferred_element_type=F32).astype(BF16)
        store(cols, k)
    for copy in sent:
        copy.wait()


def back_part(both, gate, up, downs, sets):
    rows, wide = both.shape
    width = wide // 2
    unit = gate.shape[1] // 4
    weights = [w for s in sets for w in s]
    operands = [both, gate, up, *downs, *weights]
    anywhere = pl.BlockSpec(memory_space=pl.ANY)
    near = pl.BlockSpec(memory_space=pltpu.VMEM)
    return call(
        lambda *refs: back_kernel(len(downs), *refs),
        "back_part",
        [struct((rows, width + LANES), BF16)] + [struct((rows, 4 * unit), BF16)] * 2,
        in_specs=[anywhere] * len(operands),
        out_specs=[anywhere, near, near],
        scratch_shapes=[
            pltpu.VMEM((rows, width), BF16),
            pltpu.VMEM((4 * unit, width), BF16),
            pltpu.VMEM((rows, 4 * unit), F32),
            pltpu.VMEM((rows, 4 * unit), F32),
            pltpu.VMEM((8, width, unit), BF16),
            pltpu.VMEM((rows, width + LANES), BF16),
            pltpu.SemaphoreType.DMA((2 * (1 + len(downs)) + 2 + 32,)),
            pltpu.SemaphoreType.DMA((5,)),
        ],
    )(*operands)


def tall_kernel(n_part, *refs):
    gate_ref, up_ref = refs[-2:]
    extra = refs[2 * n_part : -2]
    unit = gate_ref.shape[1]
    x = join(refs[:n_part], 0)
    d = join(refs[n_part : 2 * n_part], 0)
    out = lax.dot_general(x, d, OUTER, preferred_element_type=F32)
    gate, up = out[:, :unit], out[:, unit:]
    if extra:
        gate = gate + extra[0][...].astype(F32)
        up = up + extra[1][...].astype(F32)
    gate_ref[...] = gate.astype(BF16)
    up_ref[...] = up.astype(BF16)


def tall_part(xs, ds, unit, start, steps, rows, addends=(), into=(), flops=0):
    n = len(xs) + len(ds) + len(addends)
    full = rows > steps * PIECE
    return call(
        lambda *refs: tall_kernel(len(xs), *refs[:n], *refs[-2:]),
        "tall_part",
        [struct((rows, unit), BF16)] * 2,
        grid=(steps,),
        in_specs=[
            pl.BlockSpec(
                (x.shape[0], PIECE), lambda i, far=x.shape[1] == FAR * PIECE: (0, i if far else start + i)
            )
            for x in xs
        ]
        + [pl.BlockSpec((d.shape[0], 2 * unit), lambda i, at=at: (0, at)) for d, at in ds]
        + [pl.BlockSpec((PIECE, unit), lambda i: (i, 0))] * len(addends)
        + [pl.BlockSpec(memory_space=pl.ANY)] * len(into),
        out_specs=[pl.BlockSpec((PIECE, unit), lambda i: (start + i if full else i, 0))] * 2,
        input_output_aliases={n + k: k for k in range(len(into))},
        flops=flops,
    )(*xs, *[d for d, _ in ds], *addends, *into)


def flat_kernel(y0, y1, s0, s1, *rest):
    down_ref = rest[-1]
    y = jnp.concatenate([y0[...], y1[...]], 0)
    s = jnp.concatenate([s0[...], s1[...]], 0)
    out = lax.dot_general(s, y, OUTER, preferred_element_type=F32)
    if len(rest) > 1:
        out = out + rest[0][...].astype(F32)
    down_ref[...] = out.astype(BF16)


def flat_part(both, s, which, addend=None, flops=0):
    rows, wide = both[0].shape
    width = wide // 2
    unit = s[0].shape[1] // 2
    steps = width // BLOCK
    y_spec = pl.BlockSpec((rows, BLOCK), lambda i: (0, i + steps))
    s_spec = pl.BlockSpec((rows, unit), lambda i: (0, which))
    o_spec = pl.BlockSpec((unit, BLOCK), lambda i: (0, i))
    extra = () if addend is None else (addend,)
    return call(
        flat_kernel,
        "flat_part",
        struct((unit, width), BF16),
        grid=(steps,),
        in_specs=[y_spec] * 2 + [s_spec] * 2 + [o_spec] * len(extra),
        out_specs=o_spec,
        flops=flops,
    )(*both, *s, *extra)


def flip(value, axis):
    count = lax.axis_size(axis)
    return lax.ppermute(value, axis, [(i, i ^ 1) for i in range(count)])


def after(value, first):
    return lax.optimization_barrier((value, first))[0]


def body(tokens_in, grad_out, router_logit, expert_index, gate_half, up_half, down_half):
    n_ctx = lax.axis_size("ctx")
    n_tp = lax.axis_size("tp")
    logit = router_logit[None]
    route = expert_index.reshape(1, -1)
    send, place = spread(tokens_in, grad_out, logit, route, n_ctx * n_tp)
    recv = lax.all_to_all(send, ("ctx", "tp"), split_axis=0, concat_axis=0, tiled=True)
    mine = arrange(recv, tokens_in.shape[1], n_ctx, n_tp)
    own = (gate_half[0], up_half[0], down_half[0])
    cut = 3 * PAD
    far_mine = flip(mine[:, : FAR * PIECE], "tp")
    gate, down = after((own[0], own[2]), recv)
    up, first, second, far_mine = lax.optimization_barrier(
        (own[1], down[:cut], down[cut:], far_mine)
    )
    across = lambda group: tuple(flip(w, "core") for w in group)
    other = (flip(gate, "tp"), flip(up, "tp"))
    own_there = across(own)
    gate_there = flip(other[0], "core")
    first, own_there, gate_there = lax.optimization_barrier((first, own_there, gate_there))
    most, late = flip(first, "tp"), flip(second, "tp")
    sets = (own[:2], other, own_there[:2], (gate_there, flip(other[1], "core")))
    here = lax.all_gather(mine, "z", axis=0, tiled=True)
    here, sets, most = lax.optimization_barrier((here, sets, most))
    beside = flip(here, "core")
    both = (here, beside)
    s_here, s_there, gate, up = gate_up_part(here, sets)
    s = (s_here, flip(s_there, "core"))
    give_down = flat_part(both, s, 1)
    got_down = flip(give_down, "tp")
    most = after(most, s_here)
    late = after(late, give_down)
    downs = (own[2], most, late, own_there[2], flip(most, "core"), flip(late, "core"))
    part, d_here, d_there = back_part(after(here, give_down), gate, up, downs, sets)
    far = lax.all_gather(far_mine, "z", axis=0, tiled=True)
    part, far = lax.optimization_barrier((part, far))
    summed = lax.optimization_barrier(
        lax.psum_scatter(part, "z", scatter_dimension=0, tiled=True)
    )
    far_beside = flip(far, "core")
    d = after((d_here, flip(d_there, "core")), part)
    width, unit = own[0].shape
    steps = width // PIECE - FAR
    give = tall_part(both, [(w, 1) for w in d], unit, FAR, steps, steps * PIECE)
    got = (flip(give[0], "tp"), flip(give[1], "tp"))
    far_d = flip(jnp.concatenate([w[:, 2 * unit :] for w in d], 0), "tp")
    s, d, got_down = lax.optimization_barrier((s, after(d, give[0]), got_down))
    down_grad = flat_part(both, s, 0, got_down, SHORT)
    d, far_d = after((d, far_d), down_grad)
    around = both + (far, far_beside)
    d_all = [(w, 0) for w in (*d, *jnp.split(far_d, 2))]
    top = tall_part(around, d_all, unit, 0, FAR, width, flops=SHORT)
    tall_grads = tall_part(both, d_all[:2], unit, FAR, steps, width, got, top)
    summed = after(summed, top[0])
    shipped = ship(summed, n_ctx, n_tp)
    landed = lax.all_to_all(shipped, ("ctx", "tp"), split_axis=0, concat_axis=0, tiled=True)
    input_grad, logit_grad = take_home(landed, place, logit, tokens_in.shape[1])
    return input_grad, logit_grad[0], tall_grads[0][None], tall_grads[1][None], down_grad[None]


def solution(mesh):
    n_dp = mesh.shape["dp"]
    fine = Mesh(
        mesh.devices.reshape(n_dp // 2, 2, mesh.shape["ctx"], mesh.shape["tp"]),
        ("z", "core", "ctx", "tp"),
    )
    dp = ("z", "core")
    token = dp + ("ctx",)
    in_specs = (
        P(token, "tp"),
        P(token, "tp"),
        P(token),
        P(token, None),
        P(("ctx", "tp"), None, dp),
        P(("ctx", "tp"), None, dp),
        P(("ctx", "tp"), dp, None),
    )
    out_specs = (
        P(token, "tp"),
        P(token),
        P(("ctx", "tp"), None, dp),
        P(("ctx", "tp"), None, dp),
        P(("ctx", "tp"), dp, None),
    )
    return jax.shard_map(body, mesh=fine, in_specs=in_specs, out_specs=out_specs, check_vma=False)
```
